256 devices in a mesh: sub: 16 (over x, y), dev: 16 (over z, core).
Axes of the slice: x: 4, y: 4, z: 8, core: 2. Of those that a mesh axis runs over, the one named last changes fastest.
Arguments:
- pressure: float32 [1024, 512, 256], P('sub', 'dev'), may hold values from -6 to 6
- storage: float32 [1024, 512, 256], P('sub', 'dev'), may hold values from 0.5 to 4
- source: float32 [1024, 512, 256], P('sub', 'dev'), may hold values from -6 to 6
- left_data: float32 [16, 4, 512, 256], P('sub', None, 'dev'), may hold values from -6 to 6
- right_data: float32 [16, 4, 512, 256], P('sub', None, 'dev'), may hold values from -6 to 6
- widths: int32 [16], P('sub'), may hold values from 32 to 64, as said below
Outputs:
- pressure_end: float32 [1024, 512, 256], P('sub', 'dev')
- new_left: float32 [16, 4, 512, 256], P('sub', None, 'dev')
- new_right: float32 [16, 4, 512, 256], P('sub', None, 'dev')
The draws below stay inside these ranges and needn't reach their ends.
Inputs may be any that keep to these rules, and one draw needn't show every extreme that they name: `widths`: each subdomain has 32 to 64 live planes; in every draw some subdomain has exactly 64 and another exactly 32.
All inputs are finite; a program needn't handle non-finite values.
Results may differ from the reference program's by a relative error of at most 0.0003.
Values sent between devices are 32-bit elements; how exact they have to be, the bound alone decides.
No kernel may reach another device: no remote copies, remote signals or barrier semaphores. Data moves between devices by JAX's collectives and lax.ppermute only.
A program may use at most 128 MiB of HBM per device.

```python
import math
import jax
import jax.numpy as jnp
from jax import lax

PLANES = 64
NZ = 256
STEPS = 4
NX = 1024
NY = 512
N_SUB = 16


def draw_widths(key, part):
    key = jax.random.fold_in(key, 7)
    key_vals, key_order = jax.random.split(key)
    values = jax.random.randint(key_vals, (N_SUB,), PLANES // 2, PLANES + 1).astype(jnp.int32)
    order = jax.random.permutation(key_order, N_SUB)
    values = values.at[order[0]].set(PLANES)
    values = values.at[order[1]].set(PLANES // 2)
    return values.astype(jnp.int32)


def levels(stream_key, extent, cuts, smallest, high):
    gain, own = 1.0, jax.random.fold_in(stream_key, 6)
    for dim, shards_of in cuts:
        draws = jnp.exp(jax.random.uniform(jax.random.fold_in(own, dim), (shards_of,), jnp.float32, smallest / len(cuts), high / len(cuts)))
        gain = gain * jnp.repeat(draws, extent[dim] // shards_of).reshape([-1 if axis == dim else 1 for axis in range(len(extent))])
    return gain


def gaussian(key, shape, deviation, most, shards=(), kind=jnp.bfloat16):
    values = deviation * jax.random.normal(key, shape, jnp.float32)
    if shards:
        values = values * levels(key, shape, shards, -0.22, 0.18)
    return jnp.clip(values, -most, most).astype(kind)


def setup_inputs(seed: int = 0) -> dict:
    key_list = jax.random.split(jax.random.key(seed), 7)
    pressure = gaussian(key_list[0], (NX, NY, NZ), 1.0, 6.0, ((0, 16), (1, 16)), jnp.float32)
    storage = jnp.clip(jnp.exp(math.log(4.0) - 2.0794415 * jax.random.uniform(key_list[1], (NX, NY, NZ), jnp.float32) ** levels(key_list[1], (NX, NY, NZ), ((0, 16), (1, 16)), -0.2, 0.2)), 0.5, 4.0)
    source = gaussian(key_list[2], (NX, NY, NZ), 1.0, 6.0, ((0, 16), (1, 16)), jnp.float32)
    left_data = gaussian(key_list[3], (N_SUB, STEPS, NY, NZ), 1.0, 6.0, ((0, 16), (2, 16)), jnp.float32)
    right_data = gaussian(key_list[4], (N_SUB, STEPS, NY, NZ), 1.0, 6.0, ((0, 16), (2, 16)), jnp.float32)
    widths = draw_widths(jax.random.fold_in(key_list[6], 71), 0)
    return dict(pressure=pressure, storage=storage, source=source, left_data=left_data, right_data=right_data, widths=widths)


BETA = 1.5
RHO_ZERO = 0.9
RHO_ONE = 1.0 / (2.0 / 0.9 - 0.9)
COEF_ONE = RHO_ONE * RHO_ZERO
COEF_TWO = 2.0 * RHO_ONE / 0.9


def neighbours(padded):
    along_x = padded[2:, 1:-1, 1:-1] + padded[:-2, 1:-1, 1:-1]
    along_y = padded[1:-1, 2:, 1:-1] + padded[1:-1, :-2, 1:-1]
    along_z = padded[1:-1, 1:-1, 2:] + padded[1:-1, 1:-1, :-2]
    return (along_x + along_y) + along_z


def solve_group(items):
    start, storage, source, left_in, right_in, width = items
    planes = jnp.arange(start.shape[0], dtype=jnp.int32)[:, None, None]
    live = (planes < width).astype(jnp.float32)
    first = (planes == 0).astype(jnp.float32)
    last = (planes == width - 1).astype(jnp.float32)
    diag = storage + 4.0 + jnp.where(planes == 0, BETA, 1.0) + jnp.where(planes == width - 1, BETA, 1.0)

    def operate(field):
        return (diag * field - neighbours(jnp.pad(field, 1))) * live

    field = start * live
    lefts = []
    rights = []
    for step in range(STEPS):
        rhs = (storage * field + source + first * left_in[step] + last * right_in[step]) * live
        resid_zero = rhs - operate(field)
        dir_zero = resid_zero / diag
        first_iter = field + dir_zero
        resid_one = rhs - operate(first_iter)
        dir_one = COEF_ONE * dir_zero + COEF_TWO * resid_one / diag
        field = first_iter + dir_one
        plane_a = field[0]
        plane_b = field[1]
        plane_c = lax.dynamic_slice_in_dim(field, width - 1, 1, 0)[0]
        plane_d = lax.dynamic_slice_in_dim(field, width - 2, 1, 0)[0]
        lefts.append(BETA * plane_a + (plane_a - plane_b))
        rights.append(BETA * plane_c + (plane_c - plane_d))
    return field, jnp.stack(lefts), jnp.stack(rights)


def reference(pressure, storage, source, left_data, right_data, widths):
    groups = left_data.shape[0]
    shape = (groups, PLANES) + pressure.shape[1:]
    fields, lefts, rights = lax.map(solve_group, (pressure.reshape(shape), storage.reshape(shape), source.reshape(shape), left_data, right_data, widths.astype(jnp.int32)))
    zeros = jnp.zeros_like(lefts[:1])
    new_left = jnp.concatenate([zeros, rights[:-1]], axis=0)
    new_right = jnp.concatenate([lefts[1:], zeros], axis=0)
    return fields.reshape(pressure.shape), new_left, new_right
```

```python
import jax
import jax.numpy as jnp
from jax import lax
from jax.experimental import pallas as pl
from jax.experimental.pallas import tpu as pltpu
from jax.sharding import PartitionSpec as P

BETA = 1.5
RHO_ZERO = 0.9
RHO_ONE = 1.0 / (2.0 / 0.9 - 0.9)
COEF_ONE = RHO_ONE * RHO_ZERO
COEF_TWO = 2.0 * RHO_ONE / 0.9

LANES = 128
SUB = 8
HALO = 8
PLANES = 64
ROWS = 32
STEPS = 4
TALL = ROWS + 2 * HALO
TILES = TALL // SUB
HALVES = 2
CELLS = TILES * HALVES
GROUP = 8


def along_depth(low, high, first_lane, last_lane):
    right_low = pltpu.roll(low, 1, 1)
    right_high = pltpu.roll(high, 1, 1)
    left_low = pltpu.roll(low, LANES - 1, 1)
    left_high = pltpu.roll(high, LANES - 1, 1)
    return (
        jnp.where(first_lane, 0.0, right_low) + jnp.where(last_lane, left_high, left_low),
        jnp.where(first_lane, right_low, right_high) + jnp.where(last_lane, 0.0, left_high),
    )


def sweep(field, group, emit, first_lane, last_lane):
    base = group * GROUP
    for tile in range(TILES):
        before = [field[base, 2 * tile + half] for half in range(HALVES)]
        here = [field[base + 1, 2 * tile + half] for half in range(HALVES)]
        for plane in range(GROUP):
            at = base + plane
            after = [field[at + 2, 2 * tile + half] for half in range(HALVES)]
            depth = along_depth(here[0], here[1], first_lane, last_lane)
            for half in range(HALVES):
                if tile > 0:
                    above = field[at + 1, 2 * (tile - 1) + half]
                else:
                    above = pltpu.roll(field[at + 1, 2 * (TILES - 1) + half], 1, 0)
                if tile < TILES - 1:
                    below = field[at + 1, 2 * (tile + 1) + half]
                else:
                    below = pltpu.roll(field[at + 1, half], SUB - 1, 0)
                around = ((before[half] + after[half]) + (above + below)) + depth[half]
                emit(at, 2 * tile + half, here[half], around)
            before, here = here, after


def strided(tile):
    return pl.ds(tile, SUB, stride=TILES)


def kernel(
    widths, pressure, storage, source, left, right, low, high,
    field_out, trace_high_out, trace_low_out,
    p_nat, s_nat, f_nat, l_nat, r_nat, th_nat, tl_nat,
    u_even, u_odd, x1, b, s, f, dinv, dinv_two, in_sems, out_sems,
):
    width = widths[0]
    copies = []

    def fetch(src, dst):
        copy = pltpu.make_async_copy(src, dst, in_sems.at[len(copies)])
        copy.start()
        copies.append(copy)

    for half in range(HALVES):
        lanes = pl.ds(half * LANES, LANES)
        for index, (own, nat) in enumerate(((pressure, p_nat), (storage, s_nat), (source, f_nat))):
            planes = pl.ds(index * PLANES, PLANES)
            fetch(own.at[:, :, lanes], nat.at[:, half, pl.ds(HALO, ROWS), :])
            fetch(low.at[planes, :, lanes], nat.at[:, half, pl.ds(0, HALO), :])
            fetch(high.at[planes, :, lanes], nat.at[:, half, pl.ds(HALO + ROWS, HALO), :])
        for index, (own, nat) in enumerate(((left, l_nat), (right, r_nat))):
            planes = pl.ds(3 * PLANES + index * STEPS, STEPS)
            fetch(own.at[:, :, lanes], nat.at[:, half, pl.ds(HALO, ROWS), :])
            fetch(low.at[planes, :, lanes], nat.at[:, half, pl.ds(0, HALO), :])
            fetch(high.at[planes, :, lanes], nat.at[:, half, pl.ds(HALO + ROWS, HALO), :])
    for copy in copies:
        copy.wait()

    lane = lax.broadcasted_iota(jnp.int32, (SUB, LANES), 1)
    zero = jnp.zeros((SUB, LANES), jnp.float32)
    for cell in range(CELLS):
        for plane in (0, PLANES + 1):
            u_even[plane, cell] = zero
            u_odd[plane, cell] = zero
            x1[plane, cell] = zero

    def prepare(x, _):
        live = (x < width).astype(jnp.float32)
        extra = 4.0 + jnp.where(x == 0, BETA, 1.0) + jnp.where(x == width - 1, BETA, 1.0)
        for tile in range(TILES):
            for half in range(HALVES):
                cell = 2 * tile + half
                rows = strided(tile)
                coef = s_nat[x, half, rows, :]
                u_even[x + 1, cell] = p_nat[x, half, rows, :] * live
                s[x, cell] = coef
                f[x, cell] = f_nat[x, half, rows, :]
                inverse = jnp.where(coef > 0.0, live / (coef + extra), 0.0)
                dinv[x, cell] = inverse
                dinv_two[x, cell] = COEF_TWO * inverse
        return 0

    lax.fori_loop(0, PLANES, prepare, 0)

    first_lane = lane == 0
    last_lane = lane == LANES - 1
    for step in range(STEPS):
        u, u_next = (u_even, u_odd) if step % 2 == 0 else (u_odd, u_even)
        for cell in range(CELLS):
            rows = strided(cell // 2)
            f[0, cell] = f_nat[0, cell % 2, rows, :] + l_nat[step, cell % 2, rows, :]
            f[width - 1, cell] = f_nat[width - 1, cell % 2, rows, :] + r_nat[step, cell % 2, rows, :]

        def first_half(group, _, u=u):
            def emit(x, cell, here, around):
                rhs = s[x, cell] * here + f[x, cell]
                b[x, cell] = rhs
                x1[x + 1, cell] = (rhs + around) * dinv[x, cell]

            sweep(u, group, emit, first_lane, last_lane)
            return 0

        def second_half(group, _, u=u, u_next=u_next, step=step):
            def emit(x, cell, here, around):
                value = (b[x, cell] + around) * dinv_two[x, cell] - COEF_ONE * u[x + 1, cell]
                u_next[x + 1, cell] = value
                if step == STEPS - 1:
                    p_nat[x, cell % 2, strided(cell // 2), :] = value

            sweep(x1, group, emit, first_lane, last_lane)
            return 0

        lax.fori_loop(0, PLANES // GROUP, first_half, 0)
        lax.fori_loop(0, PLANES // GROUP, second_half, 0)
        for cell in range(CELLS):
            rows = strided(cell // 2)
            at_a, at_b = u_next[1, cell], u_next[2, cell]
            at_c, at_d = u_next[width, cell], u_next[width - 1, cell]
            tl_nat[step, cell % 2, rows, :] = BETA * at_a + (at_a - at_b)
            th_nat[step, cell % 2, rows, :] = BETA * at_c + (at_c - at_d)

    outs = []
    for half in range(HALVES):
        lanes = pl.ds(half * LANES, LANES)
        for nat, out in ((th_nat, trace_high_out), (tl_nat, trace_low_out), (p_nat, field_out)):
            copy = pltpu.make_async_copy(
                nat.at[:, half, pl.ds(HALO, ROWS), :], out.at[:, :, lanes], out_sems.at[len(outs)]
            )
            copy.start()
            outs.append(copy)
    for copy in outs:
        copy.wait()


def on_device(pressure, storage, source, left_data, right_data, widths):
    left_in = left_data[0]
    right_in = right_data[0]
    arrays = (pressure, storage, source, left_in, right_in)
    count = lax.axis_size("dev")
    forward = [(i, i + 1) for i in range(count - 1)]
    backward = [(i + 1, i) for i in range(count - 1)]
    low = lax.ppermute(jnp.concatenate([a[:, ROWS - HALO :] for a in arrays]), "dev", forward)
    high = lax.ppermute(jnp.concatenate([a[:, :HALO] for a in arrays]), "dev", backward)

    anywhere = pl.BlockSpec(memory_space=pl.ANY)
    natural = pltpu.VMEM((PLANES, HALVES, TALL, LANES), jnp.float32)
    narrow = pltpu.VMEM((STEPS, HALVES, TALL, LANES), jnp.float32)
    tiled = pltpu.VMEM((PLANES, CELLS, SUB, LANES), jnp.float32)
    padded = pltpu.VMEM((PLANES + 2, CELLS, SUB, LANES), jnp.float32)
    trace = jax.ShapeDtypeStruct(left_in.shape, jnp.float32)
    field, trace_high, trace_low = pl.pallas_call(
        kernel,
        out_shape=(jax.ShapeDtypeStruct(pressure.shape, jnp.float32), trace, trace),
        in_specs=[pl.BlockSpec(memory_space=pltpu.SMEM)] + [anywhere] * 7,
        out_specs=(anywhere,) * 3,
        scratch_shapes=[
            natural, natural, natural, narrow, narrow, narrow, narrow,
            padded, padded, padded, tiled, tiled, tiled, tiled, tiled,
            pltpu.SemaphoreType.DMA((30,)), pltpu.SemaphoreType.DMA((6,)),
        ],
        compiler_params=pltpu.CompilerParams(vmem_limit_bytes=44 * 2**20),
        name="window",
    )(widths, pressure, storage, source, left_in, right_in, low, high)

    subs = lax.axis_size("sub")
    up = [(i, i + 1) for i in range(subs - 1)]
    down = [(i + 1, i) for i in range(subs - 1)]
    new_left = lax.ppermute(trace_high, "sub", up)
    new_right = lax.ppermute(trace_low, "sub", down)
    return (field, new_left[None], new_right[None])


def solution(mesh):
    in_specs = (
        P("sub", "dev", None),
        P("sub", "dev", None),
        P("sub", "dev", None),
        P("sub", None, "dev", None),
        P("sub", None, "dev", None),
        P("sub"),
    )
    out_specs = (P("sub", "dev", None), P("sub", None, "dev", None), P("sub", None, "dev", None))
    return jax.shard_map(
        on_device, mesh=mesh, in_specs=in_specs, out_specs=out_specs, check_vma=False
    )
```

```python
import functools

import jax
import jax.numpy as jnp
from jax import lax
from jax.experimental import pallas as pl
from jax.experimental.pallas import tpu as pltpu
from jax.sharding import PartitionSpec as P

BETA = 1.5
RHO_ZERO = 0.9
RHO_ONE = 1.0 / (2.0 / 0.9 - 0.9)
COEF_ONE = RHO_ONE * RHO_ZERO
COEF_TWO = 2.0 * RHO_ONE / 0.9

LANES = 128
SUB = 8
HALVES = 2
HALO = 8
PLANES = 64
ROWS = 32
STEPS = 4
GROUP = 8
CHUNKS = 4
PACK_BYTES = 57 * 2**20
WINDOW_BYTES = 50 * 2**20


def along_depth(low, high, first_lane, last_lane):
    right_low = pltpu.roll(low, 1, 1)
    right_high = pltpu.roll(high, 1, 1)
    left_low = pltpu.roll(low, LANES - 1, 1)
    left_high = pltpu.roll(high, LANES - 1, 1)
    return (
        jnp.where(first_lane, 0.0, right_low) + jnp.where(last_lane, left_high, left_low),
        jnp.where(first_lane, right_low, right_high) + jnp.where(last_lane, 0.0, left_high),
    )


def sweep(tiles, field, group, emit, first_lane, last_lane):
    cells = tiles * HALVES
    base = group * GROUP
    before = [field[base, cell] for cell in range(cells)]
    here = [field[base + 1, cell] for cell in range(cells)]
    for plane in range(GROUP):
        at = base + plane
        after = [field[at + 2, cell] for cell in range(cells)]
        for tile in range(tiles):
            depth = along_depth(here[2 * tile], here[2 * tile + 1], first_lane, last_lane)
            for half in range(HALVES):
                cell = 2 * tile + half
                if tile > 0:
                    above = here[cell - 2]
                else:
                    above = pltpu.roll(here[cells - 2 + half], 1, 0)
                if tile < tiles - 1:
                    below = here[cell + 2]
                else:
                    below = pltpu.roll(here[half], SUB - 1, 0)
                around = ((before[cell] + after[cell]) + (above + below)) + depth[half]
                emit(at, cell, here[cell], around)
        before, here = here, after


def pack_kernel(pressure, storage, source, left, right, off_chip, on_chip, sems):
    odd = lax.rem(lax.axis_index("dev"), 2)
    copies = []
    for out, row in ((off_chip, odd * (ROWS - HALO)), (on_chip, (1 - odd) * (ROWS - HALO))):
        rows = pl.ds(pl.multiple_of(row, SUB), HALO)
        at = 0
        for own in (pressure, storage, source, left, right):
            planes = own.shape[0]
            copy = pltpu.make_async_copy(
                own.at[:, rows, :], out.at[pl.ds(at, planes)], sems.at[len(copies)]
            )
            copy.start()
            copies.append(copy)
            at += planes
    for copy in copies:
        copy.wait()


def window_kernel(
    tiles, own_rows, halo_at_end, kept_rows, aliased,
    widths, pressure, storage, source, left, right, halo, *rest,
):
    if aliased:
        rest = rest[3:]
    (
        field_out, trace_high_out, trace_low_out,
        p_nat, s_nat, f_nat, l_nat, r_nat, th_nat, tl_nat,
        u_even, u_odd, x1, b, s, f, dinv, dinv_two, in_sems, out_sems,
    ) = rest
    cells = tiles * HALVES
    width = widths[0]
    odd = lax.rem(lax.axis_index("dev"), 2)
    at_end = odd if halo_at_end == 1 else 1 - odd
    own_src = pl.ds(pl.multiple_of(at_end * (ROWS - own_rows), SUB), own_rows)
    own_dst = pl.ds(pl.multiple_of((1 - at_end) * HALO, SUB), own_rows)
    halo_dst = pl.ds(pl.multiple_of(at_end * own_rows, SUB), HALO)
    kept_src = pl.ds(HALO, kept_rows)
    kept_dst = pl.ds(pl.multiple_of(at_end * (ROWS - kept_rows), SUB), kept_rows)

    count = 0

    def fetch(own, nat, size, start, offset):
        nonlocal count
        copies = []
        for half in range(HALVES):
            lanes = pl.ds(half * LANES, LANES)
            planes = pl.ds(start, size)
            for src, dst in (
                (own.at[planes, own_src, lanes], nat.at[planes, half, own_dst, :]),
                (halo.at[pl.ds(offset + start, size), :, lanes], nat.at[planes, half, halo_dst, :]),
            ):
                copy = pltpu.make_async_copy(src, dst, in_sems.at[count])
                copy.start()
                copies.append(copy)
                count += 1
        return copies

    size = PLANES // CHUNKS
    waits = []
    for chunk in range(CHUNKS):
        waits.append([])
        for index, (own, nat) in enumerate(((pressure, p_nat), (storage, s_nat), (source, f_nat))):
            waits[chunk] += fetch(own, nat, size, chunk * size, index * PLANES)
    last_waits = fetch(left, l_nat, STEPS, 0, 3 * PLANES)
    last_waits += fetch(right, r_nat, STEPS, 0, 3 * PLANES + STEPS)

    lane = lax.broadcasted_iota(jnp.int32, (SUB, LANES), 1)
    first_lane = lane == 0
    last_lane = lane == LANES - 1
    zero = jnp.zeros((SUB, LANES), jnp.float32)
    for cell in range(cells):
        for plane in (0, PLANES + 1):
            u_even[plane, cell] = zero
            u_odd[plane, cell] = zero
            x1[plane, cell] = zero

    def strided(tile):
        return pl.ds(tile, SUB, stride=tiles)

    def prepare(x, _):
        live = (x < width).astype(jnp.float32)
        extra = 4.0 + jnp.where(x == 0, BETA, 1.0) + jnp.where(x == width - 1, BETA, 1.0)
        for cell in range(cells):
            half, rows = cell % 2, strided(cell // 2)
            coef = s_nat[x, half, rows, :]
            u_even[x + 1, cell] = p_nat[x, half, rows, :] * live
            s[x, cell] = coef
            f[x, cell] = f_nat[x, half, rows, :]
            inverse = jnp.where(coef > 0.0, live / (coef + extra), 0.0)
            dinv[x, cell] = inverse
            dinv_two[x, cell] = COEF_TWO * inverse
        return 0

    for chunk in range(CHUNKS):
        for copy in waits[chunk]:
            copy.wait()
        lax.fori_loop(chunk * size, (chunk + 1) * size, prepare, 0)
    for copy in last_waits:
        copy.wait()

    for step in range(STEPS):
        u, u_next = (u_even, u_odd) if step % 2 == 0 else (u_odd, u_even)
        for cell in range(cells):
            half, rows = cell % 2, strided(cell // 2)
            f[0, cell] = f_nat[0, half, rows, :] + l_nat[step, half, rows, :]
            f[width - 1, cell] = f_nat[width - 1, half, rows, :] + r_nat[step, half, rows, :]

        def first_half(group, _, u=u):
            def emit(x, cell, here, around):
                rhs = s[x, cell] * here + f[x, cell]
                b[x, cell] = rhs
                x1[x + 1, cell] = (rhs + around) * dinv[x, cell]

            sweep(tiles, u, group, emit, first_lane, last_lane)
            return 0

        def second_half(group, _, u=u, u_next=u_next, step=step):
            def emit(x, cell, here, around):
                value = (b[x, cell] + around) * dinv_two[x, cell] - COEF_ONE * u[x + 1, cell]
                u_next[x + 1, cell] = value
                if step == STEPS - 1:
                    p_nat[x, cell % 2, strided(cell // 2), :] = value

            sweep(tiles, x1, group, emit, first_lane, last_lane)
            return 0

        lax.fori_loop(0, PLANES // GROUP, first_half, 0)
        lax.fori_loop(0, PLANES // GROUP, second_half, 0)
        for cell in range(cells):
            half, rows = cell % 2, strided(cell // 2)
            at_a, at_b = u_next[1, cell], u_next[2, cell]
            at_c, at_d = u_next[width, cell], u_next[width - 1, cell]
            tl_nat[step, half, rows, :] = BETA * at_a + (at_a - at_b)
            th_nat[step, half, rows, :] = BETA * at_c + (at_c - at_d)

    outs = []
    for half in range(HALVES):
        lanes = pl.ds(half * LANES, LANES)
        for nat, out in ((th_nat, trace_high_out), (tl_nat, trace_low_out), (p_nat, field_out)):
            copy = pltpu.make_async_copy(
                nat.at[:, half, kept_src, :], out.at[:, kept_dst, lanes], out_sems.at[len(outs)]
            )
            copy.start()
            outs.append(copy)
    for copy in outs:
        copy.wait()


ANYWHERE = pl.BlockSpec(memory_space=pl.ANY)
IN_HBM = pl.BlockSpec(memory_space=pltpu.HBM)


def run_window(tiles, own_rows, halo_at_end, kept_rows, name, args, previous=()):
    rows = tiles * SUB
    cells = tiles * HALVES
    natural = pltpu.VMEM((PLANES, HALVES, rows, LANES), jnp.float32)
    narrow = pltpu.VMEM((STEPS, HALVES, rows, LANES), jnp.float32)
    tiled = pltpu.VMEM((PLANES, cells, SUB, LANES), jnp.float32)
    padded = pltpu.VMEM((PLANES + 2, cells, SUB, LANES), jnp.float32)
    pressure, left = args[1], args[4]
    field = jax.ShapeDtypeStruct(pressure.shape, jnp.float32)
    trace = jax.ShapeDtypeStruct(left.shape, jnp.float32)
    return pl.pallas_call(
        functools.partial(
            window_kernel, tiles, own_rows, halo_at_end, kept_rows, bool(previous)
        ),
        out_shape=(field, trace, trace),
        in_specs=[pl.BlockSpec(memory_space=pltpu.SMEM)] + [IN_HBM] * 5 + [ANYWHERE] * (1 + len(previous)),
        out_specs=(ANYWHERE,) * 3,
        input_output_aliases={7 + i: i for i in range(len(previous))},
        scratch_shapes=[
            natural, natural, natural, narrow, narrow, narrow, narrow,
            padded, padded, padded, tiled, tiled, tiled, tiled, tiled,
            pltpu.SemaphoreType.DMA((12 * CHUNKS + 8,)), pltpu.SemaphoreType.DMA((6,)),
        ],
        compiler_params=pltpu.CompilerParams(vmem_limit_bytes=WINDOW_BYTES),
        cost_estimate=pl.CostEstimate(
            flops=PLANES * rows * HALVES * LANES * 22 * STEPS,
            bytes_accessed=4 * PLANES * rows * HALVES * LANES * 4,
            transcendentals=0,
        ),
        name=name,
    )(*args, *previous)


def on_device(pressure, storage, source, left_data, right_data, widths):
    left_in = left_data[0]
    right_in = right_data[0]
    arrays = (pressure, storage, source, left_in, right_in)
    edge = jax.ShapeDtypeStruct((3 * PLANES + 2 * STEPS, HALO, pressure.shape[2]), jnp.float32)
    off_chip, on_chip = pl.pallas_call(
        pack_kernel,
        out_shape=(edge, edge),
        in_specs=[IN_HBM] * 5,
        out_specs=(ANYWHERE,) * 2,
        scratch_shapes=[pltpu.SemaphoreType.DMA((10,))],
        compiler_params=pltpu.CompilerParams(vmem_limit_bytes=PACK_BYTES),
        name="pack",
    )(*arrays)
    count = lax.axis_size("dev")
    chips = [(i, i + 1) for i in range(1, count - 1, 2)]
    cores = [(i, i + 1) for i in range(0, count, 2)]
    off_chip = lax.ppermute(off_chip, "dev", chips + [(j, i) for i, j in chips])
    on_chip = lax.ppermute(on_chip, "dev", cores + [(j, i) for i, j in cores])

    inner = run_window(5, ROWS, 0, ROWS - HALO, "inner", (widths, *arrays, on_chip))
    field, trace_high, trace_low = run_window(
        3, 2 * HALO, 1, HALO, "outer", (widths, *arrays, off_chip), inner
    )

    subs = lax.axis_size("sub")
    up = [(i, i + 1) for i in range(subs - 1)]
    down = [(i + 1, i) for i in range(subs - 1)]
    new_left = lax.ppermute(trace_high, "sub", up)
    new_right = lax.ppermute(trace_low, "sub", down)
    return (field, new_left[None], new_right[None])


def solution(mesh):
    in_specs = (
        P("sub", "dev", None),
        P("sub", "dev", None),
        P("sub", "dev", None),
        P("sub", None, "dev", None),
        P("sub", None, "dev", None),
        P("sub"),
    )
    out_specs = (P("sub", "dev", None), P("sub", None, "dev", None), P("sub", None, "dev", None))
    return jax.shard_map(
        on_device, mesh=mesh, in_specs=in_specs, out_specs=out_specs, check_vma=False
    )
```

```python
import functools

import jax
import jax.numpy as jnp
from jax import lax
from jax.experimental import pallas as pl
from jax.experimental.pallas import tpu as pltpu
from jax.sharding import PartitionSpec as P

BETA = 1.5
RHO_ZERO = 0.9
RHO_ONE = 1.0 / (2.0 / 0.9 - 0.9)
COEF_TWO = 2.0 * RHO_ONE / 0.9
ROOT = COEF_TWO**0.5

LANES = 128
SUB = 8
HALVES = 2
DEPTH = HALVES * LANES
HALO = 8
PLANES = 64
ROWS = 32
STEPS = 4
REACH = 10
PART = 16
MIDDLE = PLANES - 2 * PART
PREPARED = 4
PACK_BYTES = 60 * 2**20
WINDOW_BYTES = 50 * 2**20


def rotated_sum(low, high, first_lane, last_lane):
    right_low = pltpu.roll(low, 1, 1)
    right_high = pltpu.roll(high, 1, 1)
    left_low = pltpu.roll(low, LANES - 1, 1)
    left_high = pltpu.roll(high, LANES - 1, 1)
    return (
        jnp.where(first_lane, 0.0, right_low) + jnp.where(last_lane, left_high, left_low),
        jnp.where(first_lane, right_low, right_high) + jnp.where(last_lane, 0.0, left_high),
    )


def place(cell):
    return pl.ds(SUB * (cell // 2), SUB), pl.ds(LANES * (cell % 2), LANES)


def sweep(tiles, rotated, planes, group_planes, field, band, depth, emit, finish=None):
    cells = tiles * HALVES
    others = tiles - rotated
    size = group_planes * others * SUB

    def load(plane, cell):
        return field[(plane, *place(cell % cells))]

    def body(group, _):
        base = group * group_planes
        lane = lax.broadcasted_iota(jnp.int32, (SUB, LANES), 1)
        first_lane = lane == 0
        last_lane = lane == LANES - 1
        block = field[pl.ds(base + 1, group_planes), pl.ds(rotated * SUB, others * SUB), :]
        block = block.reshape(size, DEPTH)
        coarse = block.astype(jnp.bfloat16)
        fine = (block - coarse.astype(jnp.float32)).astype(jnp.bfloat16)
        parts = jnp.concatenate([coarse, fine], axis=0)
        sums = jnp.dot(parts, band[...], preferred_element_type=jnp.float32)
        depth[...] = sums[:size] + sums[size:]
        for tile in range(tiles):
            pair = [2 * tile + half for half in range(HALVES)]
            before = [load(base, cell) for cell in pair]
            here = [load(base + 1, cell) for cell in pair]
            for plane in range(group_planes):
                at = base + plane
                after = [load(at + 2, cell) for cell in pair]
                if tile < rotated:
                    along = rotated_sum(here[0], here[1], first_lane, last_lane)
                else:
                    rows = pl.ds((plane * others + tile - rotated) * SUB, SUB)
                    along = [depth[rows, pl.ds(half * LANES, LANES)] for half in range(HALVES)]
                for half, cell in enumerate(pair):
                    above = load(at + 1, cell - 2)
                    if tile == 0:
                        above = pltpu.roll(above, 1, 0)
                    below = load(at + 1, cell + 2)
                    if tile == tiles - 1:
                        below = pltpu.roll(below, SUB - 1, 0)
                    around = ((before[half] + after[half]) + (above + below)) + along[half]
                    emit(at, cell, here[half], around)
                before, here = here, after
        if finish is not None:
            finish(group)
        return 0

    lax.fori_loop(0, planes // group_planes, body, 0)


def pack_kernel(
    widths, pressure, storage, source, left, right, edge, middle, on_chip,
    edge_hold, middle_hold, on_hold, in_sems, out_sems,
):
    odd = lax.rem(lax.axis_index("dev"), 2)
    off_rows = pl.ds(pl.multiple_of(odd * (ROWS - HALO), SUB), HALO)
    on_rows = pl.ds(pl.multiple_of((1 - odd) * (ROWS - HALO), SUB), HALO)
    fields = (pressure, storage, source)
    everything = [(own, 0, own.shape[0]) for own in (*fields, left, right)]
    ends = [(own, at, PART) for own in fields for at in (0, widths[0] - PART)]
    ends += [(own, 0, STEPS) for own in (left, right)]
    moves = []
    for out, hold, rows, parts in (
        (edge, edge_hold, off_rows, ends),
        (on_chip, on_hold, on_rows, everything),
        (middle, middle_hold, off_rows, [(own, PART, MIDDLE) for own in fields]),
    ):
        at = 0
        for own, start, count in parts:
            index = len(moves)
            into = pl.ds(at, count)
            fetch = pltpu.make_async_copy(
                own.at[pl.ds(start, count), rows, :], hold.at[into], in_sems.at[index]
            )
            fetch.start()
            moves.append((fetch, pltpu.make_async_copy(hold.at[into], out.at[into], out_sems.at[index])))
            at += count
    for fetch, put in moves:
        fetch.wait()
        put.start()
    for fetch, put in moves:
        put.wait()


def window_kernel(kind, tiles, rotated, group_planes, own_rows, widths, *refs):
    refs = iter(refs)

    def take(count):
        return [next(refs) for _ in range(count)]

    fields = take(3)
    sides = take(2)
    halos = take(2 if kind == "outer" else 1)
    with_field, with_traces = kind != "corner", kind != "outer"
    take({"inner": 0, "corner": 2, "outer": 2}[kind])
    field_out = take(1)[0] if with_field else None
    trace_outs = take(2) if with_traces else []
    naturals = take(3)
    side_naturals = take(2)
    out_nat = take(1)[0] if with_field else None
    trace_nats = take(2) if with_traces else []
    u_even, u_odd, change, f, inverse, band, depth, in_sems, out_sems = take(9)

    cells = tiles * HALVES
    planes = 2 * REACH if kind == "corner" else PLANES
    kept_rows = ROWS - HALO if kind == "inner" else HALO
    true_width = widths[0]
    width = planes if kind == "corner" else true_width
    odd = lax.rem(lax.axis_index("dev"), 2)
    at_end = 1 - odd if kind == "inner" else odd
    own_src = pl.ds(pl.multiple_of(at_end * (ROWS - own_rows), SUB), own_rows)
    own_dst = pl.ds(pl.multiple_of((1 - at_end) * HALO, SUB), own_rows)
    halo_dst = pl.ds(pl.multiple_of(at_end * own_rows, SUB), HALO)
    kept_src = pl.ds(HALO, kept_rows)
    kept_dst = pl.ds(pl.multiple_of(at_end * (ROWS - kept_rows), SUB), kept_rows)

    used = 0

    def fetch(src, src_start, src_rows, dst, dst_start, dst_rows, count):
        nonlocal used
        copies = []
        for half in range(HALVES):
            copy = pltpu.make_async_copy(
                src.at[pl.ds(src_start, count), src_rows, pl.ds(half * LANES, LANES)],
                dst.at[pl.ds(dst_start, count), half, dst_rows, :],
                in_sems.at[used],
            )
            copy.start()
            copies.append(copy)
            used += 1
        return copies

    whole = pl.ds(0, HALO)
    chunks = 1 if kind == "corner" else 4
    size = planes // chunks
    waits = [[] for _ in range(chunks)]
    late = []
    for chunk in range(chunks):
        for index, (own, nat) in enumerate(zip(fields, naturals)):
            if kind == "corner":
                waits[0] += fetch(own, 0, own_src, nat, 0, own_dst, REACH)
                waits[0] += fetch(own, true_width - REACH, own_src, nat, REACH, own_dst, REACH)
                at = 2 * index * PART
                waits[0] += fetch(halos[0], at, whole, nat, 0, halo_dst, REACH)
                waits[0] += fetch(halos[0], at + 2 * PART - REACH, whole, nat, REACH, halo_dst, REACH)
            else:
                at = chunk * size
                waits[chunk] += fetch(own, at, own_src, nat, at, own_dst, size)
                if kind == "inner":
                    waits[chunk] += fetch(halos[0], index * planes + at, whole, nat, at, halo_dst, size)
                elif chunk == 0:
                    waits[0] += fetch(halos[0], 2 * index * PART, whole, nat, 0, halo_dst, PART)
                    waits[0] += fetch(halos[1], index * MIDDLE, whole, nat, PART, halo_dst, MIDDLE)
    side_waits = []
    side_at = 3 * (PLANES if kind == "inner" else 2 * PART)
    for index, (own, nat) in enumerate(zip(sides, side_naturals)):
        side_waits += fetch(own, 0, own_src, nat, 0, own_dst, STEPS)
        side_waits += fetch(halos[0], side_at + index * STEPS, whole, nat, 0, halo_dst, STEPS)

    row_at = lax.broadcasted_iota(jnp.int32, (DEPTH, DEPTH), 0)
    column_at = lax.broadcasted_iota(jnp.int32, (DEPTH, DEPTH), 1)
    band[...] = jnp.where(jnp.abs(row_at - column_at) == 1, 1.0, 0.0).astype(jnp.bfloat16)
    for plane in (0, planes + 1):
        for field in (u_even, u_odd, change):
            field[plane] = jnp.zeros((tiles * SUB, DEPTH), jnp.float32)

    def strided(tile):
        return pl.ds(tile, SUB, stride=tiles)

    def own_part(x):
        return 4.0 + jnp.where(x == 0, BETA, 1.0) + jnp.where(x == width - 1, BETA, 1.0)

    def prepare(index, _):
        for plane in range(PREPARED):
            x = index * PREPARED + plane
            for cell in range(cells):
                half, rows = cell % 2, strided(cell // 2)
                first, coef, rate = (nat[x, half, rows, :] for nat in naturals)
                live = jnp.full((SUB, LANES), x, jnp.int32) < width
                u_even[(x + 1, *place(cell))] = jnp.where(live, first, 0.0)
                f[x, cell] = jnp.where(live, rate, 0.0)
                inside = jnp.logical_and(live, coef > 0.0)
                inverse[x, cell] = jnp.where(inside, ROOT / (coef + own_part(x)), 0.0)
        return 0

    for chunk in range(chunks):
        for copy in waits[chunk] + late:
            copy.wait()
        late = []
        if kind == "outer" and chunk == 0:
            for index, nat in enumerate(naturals):
                late += fetch(
                    halos[0], (2 * index + 1) * PART, whole, nat, true_width - PART, halo_dst, PART
                )
        lax.fori_loop(chunk * size // PREPARED, (chunk + 1) * size // PREPARED, prepare, 0)
    for copy in side_waits:
        copy.wait()

    def field_copies(index):
        part = pl.ds(index * group_planes, group_planes)
        return [
            pltpu.make_async_copy(
                out_nat.at[part, half, kept_src, :],
                field_out.at[part, kept_dst, pl.ds(half * LANES, LANES)],
                out_sems.at[4 + 2 * index + half],
            )
            for half in range(HALVES)
        ]

    def put_field(index):
        for copy in field_copies(index):
            copy.start()

    def advance(step, u, u_next):
        for cell in range(cells):
            half, rows = cell % 2, strided(cell // 2)
            for x, side in ((0, side_naturals[0]), (width - 1, side_naturals[1])):
                f[x, cell] = naturals[2][x, half, rows, :] + side[step, half, rows, :]

        def first_half(x, cell, here, around):
            rest = (f[x, cell] - own_part(x) * here) + around
            change[(x + 1, *place(cell))] = rest * inverse[x, cell]

        def second_half(x, cell, here, around):
            value = (u[(x + 1, *place(cell))] + ROOT * here) + around * inverse[x, cell]
            u_next[(x + 1, *place(cell))] = value
            if with_field and u is u_odd:
                out_nat[x, cell % 2, strided(cell // 2), :] = value

        def finish(index):
            if with_field and u is u_odd:
                pl.when(step == STEPS - 1)(lambda: put_field(index))

        sweep(tiles, rotated, planes, group_planes, u, band, depth, first_half)
        sweep(tiles, rotated, planes, group_planes, change, band, depth, second_half, finish)
        if not with_traces:
            return
        for cell in range(cells):
            half, rows = cell % 2, strided(cell // 2)
            for nat, end, inward in ((trace_nats[0], width, width - 1), (trace_nats[1], 1, 2)):
                at_end_plane = u_next[(end, *place(cell))]
                nat[step, half, rows, :] = BETA * at_end_plane + (
                    at_end_plane - u_next[(inward, *place(cell))]
                )

    def two_steps(index, _):
        advance(2 * index, u_even, u_odd)
        advance(2 * index + 1, u_odd, u_even)
        return 0

    lax.fori_loop(0, STEPS // 2, two_steps, 0)

    copies = []
    for nat, out in zip(trace_nats, trace_outs):
        for half in range(HALVES):
            copy = pltpu.make_async_copy(
                nat.at[:, half, kept_src, :],
                out.at[:, kept_dst, pl.ds(half * LANES, LANES)],
                out_sems.at[len(copies)],
            )
            copy.start()
            copies.append(copy)
    if with_field:
        for index in range(planes // group_planes):
            copies += field_copies(index)
    for copy in copies:
        copy.wait()


ANYWHERE = pl.BlockSpec(memory_space=pl.ANY)
IN_HBM = pl.BlockSpec(memory_space=pltpu.HBM)
IN_SMEM = pl.BlockSpec(memory_space=pltpu.SMEM)


def run_window(kind, tiles, rotated, group_planes, args, halos, previous=(), after=()):
    planes = 2 * REACH if kind == "corner" else PLANES
    rows = tiles * SUB
    cells = tiles * HALVES
    natural = pltpu.VMEM((planes, HALVES, rows, LANES), jnp.float32)
    narrow = pltpu.VMEM((STEPS, HALVES, rows, LANES), jnp.float32)
    tiled = pltpu.VMEM((planes, cells, SUB, LANES), jnp.float32)
    padded = pltpu.VMEM((planes + 2, rows, DEPTH), jnp.float32)
    field = jax.ShapeDtypeStruct(args[1].shape, jnp.float32)
    trace = jax.ShapeDtypeStruct(args[4].shape, jnp.float32)
    outs = {"inner": (field, trace, trace), "corner": (trace, trace), "outer": (field,)}[kind]
    return pl.pallas_call(
        functools.partial(window_kernel, kind, tiles, rotated, group_planes, rows - HALO),
        out_shape=outs,
        in_specs=[IN_SMEM] + [IN_HBM] * 5 + [ANYWHERE] * len((*halos, *previous, *after)),
        out_specs=(ANYWHERE,) * len(outs),
        input_output_aliases={6 + len(halos) + i: i for i in range(len(previous))},
        scratch_shapes=[
            *[natural] * 3, *[narrow] * 2,
            *([] if kind == "corner" else [natural]), *([] if kind == "outer" else [narrow] * 2),
            padded, padded, padded, tiled, tiled,
            pltpu.VMEM((DEPTH, DEPTH), jnp.bfloat16),
            pltpu.VMEM((group_planes * (tiles - rotated) * SUB, DEPTH), jnp.float32),
            pltpu.SemaphoreType.DMA((64,)),
            pltpu.SemaphoreType.DMA((4 + HALVES * planes // group_planes,)),
        ],
        compiler_params=pltpu.CompilerParams(vmem_limit_bytes=WINDOW_BYTES),
        cost_estimate=pl.CostEstimate(
            flops=planes * rows * DEPTH * 22 * STEPS,
            bytes_accessed=4 * planes * rows * DEPTH * 4,
            transcendentals=0,
        ),
        name=kind,
    )(*args, *halos, *previous, *after)


def on_device(pressure, storage, source, left_data, right_data, widths):
    args = (widths, pressure, storage, source, left_data[0], right_data[0])
    rims = [
        jax.ShapeDtypeStruct((planes, HALO, DEPTH), jnp.float32)
        for planes in (6 * PART + 2 * STEPS, 3 * MIDDLE, 3 * PLANES + 2 * STEPS)
    ]
    edge, middle, on_chip = pl.pallas_call(
        pack_kernel,
        out_shape=tuple(rims),
        in_specs=[IN_SMEM] + [IN_HBM] * 5,
        out_specs=(ANYWHERE,) * 3,
        scratch_shapes=[
            *[pltpu.VMEM(rim.shape, rim.dtype) for rim in rims],
            pltpu.SemaphoreType.DMA((16,)), pltpu.SemaphoreType.DMA((16,)),
        ],
        compiler_params=pltpu.CompilerParams(vmem_limit_bytes=PACK_BYTES),
        name="pack",
    )(*args)
    count = lax.axis_size("dev")
    chips = [(i, i + 1) for i in range(1, count - 1, 2)]
    chips += [(j, i) for i, j in chips]
    cores = [(i, i + 1) for i in range(0, count, 2)]
    cores += [(j, i) for i, j in cores]
    edge = lax.ppermute(edge, "dev", chips)
    on_chip = lax.ppermute(on_chip, "dev", cores)
    middle = lax.ppermute(middle, "dev", chips)

    field, trace_high, trace_low = run_window("inner", 5, 2, 16, args, (on_chip,))
    trace_high, trace_low = run_window("corner", 3, 1, 10, args, (edge,), (trace_high, trace_low))

    subs = lax.axis_size("sub")
    up = [(i, i + 1) for i in range(subs - 1)]
    down = [(i + 1, i) for i in range(subs - 1)]
    new_left = lax.ppermute(trace_high, "sub", up)
    new_right = lax.ppermute(trace_low, "sub", down)
    (field,) = run_window("outer", 3, 1, 16, args, (edge, middle), (field,), (trace_low,))
    return (field, new_left[None], new_right[None])


def solution(mesh):
    in_specs = (
        P("sub", "dev", None),
        P("sub", "dev", None),
        P("sub", "dev", None),
        P("sub", None, "dev", None),
        P("sub", None, "dev", None),
        P("sub"),
    )
    out_specs = (P("sub", "dev", None), P("sub", None, "dev", None), P("sub", None, "dev", None))
    return jax.shard_map(
        on_device, mesh=mesh, in_specs=in_specs, out_specs=out_specs, check_vma=False
    )
```

```python
import functools

import jax
import jax.numpy as jnp
from jax import lax
from jax.experimental import pallas as pl
from jax.experimental.pallas import tpu as pltpu
from jax.sharding import PartitionSpec as P

BETA = 1.5
RHO_ZERO = 0.9
RHO_ONE = 1.0 / (2.0 / 0.9 - 0.9)
COEF_TWO = 2.0 * RHO_ONE / 0.9
ROOT = COEF_TWO**0.5

LANES = 128
SUB = 8
HALVES = 2
DEPTH = HALVES * LANES
HALO = 8
PLANES = 64
ROWS = 32
STEPS = 4
REACH = 10
PART = 16
MIDDLE = PLANES - 2 * PART
PREPARED = 4
PACK_BYTES = 50 * 2**20
WINDOW_BYTES = 50 * 2**20
OUTER_BYTES = 50 * 2**20


def rotated_sum(low, high, first_lane, last_lane):
    right_low = pltpu.roll(low, 1, 1)
    right_high = pltpu.roll(high, 1, 1)
    left_low = pltpu.roll(low, LANES - 1, 1)
    left_high = pltpu.roll(high, LANES - 1, 1)
    return (
        jnp.where(first_lane, 0.0, right_low) + jnp.where(last_lane, left_high, left_low),
        jnp.where(first_lane, right_low, right_high) + jnp.where(last_lane, 0.0, left_high),
    )


def place(cell):
    return pl.ds(SUB * (cell // 2), SUB), pl.ds(LANES * (cell % 2), LANES)


def sweep(tiles, rotated, planes, group_planes, field, band, depths, emit, finish=None):
    cells = tiles * HALVES
    others = tiles - rotated
    size = group_planes * others * SUB

    def load(plane, cell):
        return field[(plane, *place(cell % cells))]

    def multiply(group, out):
        block = field[pl.ds(group * group_planes + 1, group_planes), pl.ds(rotated * SUB, others * SUB), :]
        block = block.reshape(size, DEPTH)
        coarse = block.astype(jnp.bfloat16)
        fine = (block - coarse.astype(jnp.float32)).astype(jnp.bfloat16)
        parts = jnp.concatenate([coarse, fine], axis=0)
        sums = jnp.dot(parts, band[...], preferred_element_type=jnp.float32)
        out[...] = sums[:size] + sums[size:]

    def work(group, depth):
        base = group * group_planes
        lane = lax.broadcasted_iota(jnp.int32, (SUB, LANES), 1)
        first_lane = lane == 0
        last_lane = lane == LANES - 1
        for tile in range(tiles):
            pair = [2 * tile + half for half in range(HALVES)]
            before = [load(base, cell) for cell in pair]
            here = [load(base + 1, cell) for cell in pair]
            for plane in range(group_planes):
                at = base + plane
                after = [load(at + 2, cell) for cell in pair]
                if tile < rotated:
                    along = rotated_sum(here[0], here[1], first_lane, last_lane)
                else:
                    rows = pl.ds((plane * others + tile - rotated) * SUB, SUB)
                    along = [depth[rows, pl.ds(half * LANES, LANES)] for half in range(HALVES)]
                for half, cell in enumerate(pair):
                    above = load(at + 1, cell - 2)
                    if tile == 0:
                        above = pltpu.roll(above, 1, 0)
                    below = load(at + 1, cell + 2)
                    if tile == tiles - 1:
                        below = pltpu.roll(below, SUB - 1, 0)
                    around = ((before[half] + after[half]) + (above + below)) + along[half]
                    emit(at, cell, here[half], around)
                before, here = here, after

    groups = planes // group_planes
    multiply(0, depths[0])

    def body(index, _):
        for side in range(2):
            group = 2 * index + side
            multiply(jnp.minimum(group + 1, groups - 1), depths[1 - side])
            work(group, depths[side])
        if finish is not None:
            finish(index)
        return 0

    lax.fori_loop(0, groups // 2, body, 0)


def pack_kernel(
    widths, pressure, storage, source, sides, edge, middle, on_chip, sems,
):
    odd = lax.rem(lax.axis_index("dev"), 2)
    off_rows = pl.ds(pl.multiple_of(odd * (ROWS - HALO), SUB), HALO)
    on_rows = pl.ds(pl.multiple_of((1 - odd) * (ROWS - HALO), SUB), HALO)
    fields = (pressure, storage, source)
    everything = [(own, 0, own.shape[0]) for own in (*fields, sides)]
    ends = [(own, at, PART) for own in fields for at in (0, widths[0] - PART)]
    ends.append((sides, 0, 2 * STEPS))
    moves = []
    for out, rows, parts in (
        (edge, off_rows, ends),
        (on_chip, on_rows, everything),
        (middle, off_rows, [(own, PART, MIDDLE) for own in fields]),
    ):
        at = 0
        for own, start, count in parts:
            move = pltpu.make_async_copy(
                own.at[pl.ds(start, count), rows, :], out.at[pl.ds(at, count)], sems.at[len(moves)]
            )
            move.start()
            moves.append(move)
            at += count
    for move in moves:
        move.wait()


def window_kernel(kind, tiles, rotated, group_planes, own_rows, widths, *refs):
    refs = iter(refs)

    def take(count):
        return [next(refs) for _ in range(count)]

    fields = take(3)
    sides = take(1)[0]
    halos = take(2 if kind == "outer" else 1)
    with_field, with_traces = kind != "corner", kind != "outer"
    take({"inner": 0, "corner": 2, "outer": 2}[kind])
    field_out = take(1)[0] if with_field else None
    trace_outs = take(2) if with_traces else []
    naturals = take(3)
    side_naturals = take(2)
    out_nat = take(1)[0] if with_field else None
    trace_nats = take(2) if with_traces else []
    u_even, u_odd, change, f, inverse, band, depth_a, depth_b, in_sems, out_sems = take(10)
    depths = (depth_a, depth_b)

    cells = tiles * HALVES
    planes = 2 * REACH if kind == "corner" else PLANES
    kept_rows = ROWS - HALO if kind == "inner" else HALO
    true_width = widths[0]
    width = planes if kind == "corner" else true_width
    odd = lax.rem(lax.axis_index("dev"), 2)
    at_end = 1 - odd if kind == "inner" else odd
    own_src = pl.ds(pl.multiple_of(at_end * (ROWS - own_rows), SUB), own_rows)
    own_dst = pl.ds(pl.multiple_of((1 - at_end) * HALO, SUB), own_rows)
    halo_dst = pl.ds(pl.multiple_of(at_end * own_rows, SUB), HALO)
    kept_src = pl.ds(HALO, kept_rows)
    kept_dst = pl.ds(pl.multiple_of(at_end * (ROWS - kept_rows), SUB), kept_rows)

    used = 0

    def fetch(src, src_start, src_rows, dst, dst_start, dst_rows, count):
        nonlocal used
        copies = []
        for half in range(HALVES):
            copy = pltpu.make_async_copy(
                src.at[pl.ds(src_start, count), src_rows, pl.ds(half * LANES, LANES)],
                dst.at[pl.ds(dst_start, count), half, dst_rows, :],
                in_sems.at[used],
            )
            copy.start()
            copies.append(copy)
            used += 1
        return copies

    whole = pl.ds(0, HALO)
    chunks = 1 if kind == "corner" else 2
    size = planes // chunks
    waits = [[] for _ in range(chunks)]
    late = []
    for chunk in range(chunks):
        for index, (own, nat) in enumerate(zip(fields, naturals)):
            if kind == "corner":
                waits[0] += fetch(own, 0, own_src, nat, 0, own_dst, REACH)
                waits[0] += fetch(own, true_width - REACH, own_src, nat, REACH, own_dst, REACH)
                at = 2 * index * PART
                waits[0] += fetch(halos[0], at, whole, nat, 0, halo_dst, REACH)
                waits[0] += fetch(halos[0], at + 2 * PART - REACH, whole, nat, REACH, halo_dst, REACH)
            else:
                at = chunk * size
                waits[chunk] += fetch(own, at, own_src, nat, at, own_dst, size)
                if kind == "inner":
                    waits[chunk] += fetch(halos[0], index * planes + at, whole, nat, at, halo_dst, size)
                elif chunk == 0:
                    waits[0] += fetch(halos[0], 2 * index * PART, whole, nat, 0, halo_dst, PART)
                    waits[0] += fetch(halos[1], index * MIDDLE, whole, nat, PART, halo_dst, MIDDLE)
    side_waits = []
    side_at = 3 * (PLANES if kind == "inner" else 2 * PART)
    for index, nat in enumerate(side_naturals):
        side_waits += fetch(sides, index * STEPS, own_src, nat, 0, own_dst, STEPS)
        side_waits += fetch(halos[0], side_at + index * STEPS, whole, nat, 0, halo_dst, STEPS)

    row_at = lax.broadcasted_iota(jnp.int32, (DEPTH, DEPTH), 0)
    column_at = lax.broadcasted_iota(jnp.int32, (DEPTH, DEPTH), 1)
    band[...] = jnp.where(jnp.abs(row_at - column_at) == 1, 1.0, 0.0).astype(jnp.bfloat16)
    for plane in (0, planes + 1):
        for field in (u_even, u_odd, change):
            field[plane] = jnp.zeros((tiles * SUB, DEPTH), jnp.float32)

    def strided(tile):
        return pl.ds(tile, SUB, stride=tiles)

    def own_part(x):
        return 4.0 + jnp.where(x == 0, BETA, 1.0) + jnp.where(x == width - 1, BETA, 1.0)

    def prepare(index, _):
        for plane in range(PREPARED):
            x = index * PREPARED + plane
            for cell in range(cells):
                half, rows = cell % 2, strided(cell // 2)
                first, coef, rate = (nat[x, half, rows, :] for nat in naturals)
                live = jnp.full((SUB, LANES), x, jnp.int32) < width
                u_even[(x + 1, *place(cell))] = jnp.where(live, first, 0.0)
                f[x, cell] = jnp.where(live, rate, 0.0)
                inside = jnp.logical_and(live, coef > 0.0)
                inverse[x, cell] = jnp.where(inside, ROOT / (coef + own_part(x)), 0.0)
        return 0

    for chunk in range(chunks):
        for copy in waits[chunk] + late:
            copy.wait()
        late = []
        if kind == "outer" and chunk == 0:
            for index, nat in enumerate(naturals):
                late += fetch(
                    halos[0], (2 * index + 1) * PART, whole, nat, true_width - PART, halo_dst, PART
                )
        lax.fori_loop(chunk * size // PREPARED, (chunk + 1) * size // PREPARED, prepare, 0)
    for copy in side_waits:
        copy.wait()

    def field_copies(index):
        part = pl.ds(2 * index * group_planes, 2 * group_planes)
        return [
            pltpu.make_async_copy(
                out_nat.at[part, half, kept_src, :],
                field_out.at[part, kept_dst, pl.ds(half * LANES, LANES)],
                out_sems.at[4 + 2 * index + half],
            )
            for half in range(HALVES)
        ]

    def put_field(index):
        for copy in field_copies(index):
            copy.start()

    def advance(step, u, u_next):
        for cell in range(cells):
            half, rows = cell % 2, strided(cell // 2)
            for x, side in ((0, side_naturals[0]), (width - 1, side_naturals[1])):
                f[x, cell] = naturals[2][x, half, rows, :] + side[step, half, rows, :]

        def first_half(x, cell, here, around):
            rest = (f[x, cell] - own_part(x) * here) + around
            change[(x + 1, *place(cell))] = rest * inverse[x, cell]

        def second_half(x, cell, here, around):
            value = (u[(x + 1, *place(cell))] + ROOT * here) + around * inverse[x, cell]
            u_next[(x + 1, *place(cell))] = value
            if with_field and u is u_odd:
                out_nat[x, cell % 2, strided(cell // 2), :] = value

        def finish(index):
            if with_field and u is u_odd:
                pl.when(step == STEPS - 1)(lambda: put_field(index))

        sweep(tiles, rotated, planes, group_planes, u, band, depths, first_half)
        sweep(tiles, rotated, planes, group_planes, change, band, depths, second_half, finish)
        if not with_traces:
            return
        for cell in range(cells):
            half, rows = cell % 2, strided(cell // 2)
            for nat, end, inward in ((trace_nats[0], width, width - 1), (trace_nats[1], 1, 2)):
                at_end_plane = u_next[(end, *place(cell))]
                nat[step, half, rows, :] = BETA * at_end_plane + (
                    at_end_plane - u_next[(inward, *place(cell))]
                )

    def two_steps(index, _):
        advance(2 * index, u_even, u_odd)
        advance(2 * index + 1, u_odd, u_even)
        return 0

    lax.fori_loop(0, STEPS // 2, two_steps, 0)

    copies = []
    for nat, out in zip(trace_nats, trace_outs):
        for half in range(HALVES):
            copy = pltpu.make_async_copy(
                nat.at[:, half, kept_src, :],
                out.at[:, kept_dst, pl.ds(half * LANES, LANES)],
                out_sems.at[len(copies)],
            )
            copy.start()
            copies.append(copy)
    if with_field:
        for index in range(planes // group_planes // 2):
            copies += field_copies(index)
    for copy in copies:
        copy.wait()


ANYWHERE = pl.BlockSpec(memory_space=pl.ANY)
IN_HBM = pl.BlockSpec(memory_space=pltpu.HBM)
IN_SMEM = pl.BlockSpec(memory_space=pltpu.SMEM)


def run_window(kind, tiles, rotated, group_planes, limit, args, halos, previous=(), after=()):
    planes = 2 * REACH if kind == "corner" else PLANES
    rows = tiles * SUB
    cells = tiles * HALVES
    natural = pltpu.VMEM((planes, HALVES, rows, LANES), jnp.float32)
    narrow = pltpu.VMEM((STEPS, HALVES, rows, LANES), jnp.float32)
    tiled = pltpu.VMEM((planes, cells, SUB, LANES), jnp.float32)
    padded = pltpu.VMEM((planes + 2, rows, DEPTH), jnp.float32)
    field = jax.ShapeDtypeStruct(args[1].shape, jnp.float32)
    trace = jax.ShapeDtypeStruct((STEPS, ROWS, DEPTH), jnp.float32)
    outs = {"inner": (field, trace, trace), "corner": (trace, trace), "outer": (field,)}[kind]
    return pl.pallas_call(
        functools.partial(window_kernel, kind, tiles, rotated, group_planes, rows - HALO),
        out_shape=outs,
        in_specs=[IN_SMEM] + [IN_HBM] * 3 + [ANYWHERE] * len((args[4], *halos, *previous, *after)),
        out_specs=(ANYWHERE,) * len(outs),
        input_output_aliases={5 + len(halos) + i: i for i in range(len(previous))},
        scratch_shapes=[
            *[natural] * 3, *[narrow] * 2,
            *([] if kind == "corner" else [natural]), *([] if kind == "outer" else [narrow] * 2),
            padded, padded, padded, tiled, tiled,
            pltpu.VMEM((DEPTH, DEPTH), jnp.bfloat16),
            *[pltpu.VMEM((group_planes * (tiles - rotated) * SUB, DEPTH), jnp.float32)] * 2,
            pltpu.SemaphoreType.DMA((64,)),
            pltpu.SemaphoreType.DMA((4 + planes // group_planes,)),
        ],
        compiler_params=pltpu.CompilerParams(vmem_limit_bytes=limit),
        cost_estimate=pl.CostEstimate(
            flops=planes * rows * DEPTH * 22 * STEPS,
            bytes_accessed=4 * planes * rows * DEPTH * 4,
            transcendentals=0,
        ),
        name=kind,
    )(*args, *halos, *previous, *after)


def on_device(pressure, storage, source, left_data, right_data, widths):
    sides = jnp.concatenate([left_data[0], right_data[0]])
    args = (widths, pressure, storage, source, sides)
    rims = [
        jax.ShapeDtypeStruct((planes, HALO, DEPTH), jnp.float32)
        for planes in (6 * PART + 2 * STEPS, 3 * MIDDLE, 3 * PLANES + 2 * STEPS)
    ]
    edge, middle, on_chip = pl.pallas_call(
        pack_kernel,
        out_shape=tuple(rims),
        in_specs=[IN_SMEM] + [IN_HBM] * 3 + [ANYWHERE],
        out_specs=(ANYWHERE,) * 3,
        scratch_shapes=[pltpu.SemaphoreType.DMA((16,))],
        compiler_params=pltpu.CompilerParams(vmem_limit_bytes=PACK_BYTES),
        name="pack",
    )(*args)
    count = lax.axis_size("dev")
    chips = [(i, i + 1) for i in range(1, count - 1, 2)]
    chips += [(j, i) for i, j in chips]
    cores = [(i, i + 1) for i in range(0, count, 2)]
    cores += [(j, i) for i, j in cores]
    edge = lax.ppermute(edge, "dev", chips)
    on_chip = lax.ppermute(on_chip, "dev", cores)
    middle = lax.ppermute(middle, "dev", chips)

    field, trace_high, trace_low = run_window("inner", 5, 2, 8, WINDOW_BYTES, args, (on_chip,))
    trace_high, trace_low = run_window("corner", 3, 1, 5, WINDOW_BYTES, args, (edge,), (trace_high, trace_low))

    subs = lax.axis_size("sub")
    up = [(i, i + 1) for i in range(subs - 1)]
    down = [(i + 1, i) for i in range(subs - 1)]
    new_left = lax.ppermute(trace_high, "sub", up)
    new_right = lax.ppermute(trace_low, "sub", down)
    (field,) = run_window("outer", 3, 1, 8, OUTER_BYTES, args, (edge, middle), (field,), (trace_low,))
    return (field, new_left[None], new_right[None])


def solution(mesh):
    in_specs = (
        P("sub", "dev", None),
        P("sub", "dev", None),
        P("sub", "dev", None),
        P("sub", None, "dev", None),
        P("sub", None, "dev", None),
        P("sub"),
    )
    out_specs = (P("sub", "dev", None), P("sub", None, "dev", None), P("sub", None, "dev", None))
    return jax.shard_map(
        on_device, mesh=mesh, in_specs=in_specs, out_specs=out_specs, check_vma=False
    )
```

```python
import functools

import jax
import jax.numpy as jnp
from jax import lax
from jax.experimental import pallas as pl
from jax.experimental.pallas import tpu as pltpu
from jax.sharding import PartitionSpec as P

BETA = 1.5
RHO_ZERO = 0.9
RHO_ONE = 1.0 / (2.0 / 0.9 - 0.9)
COEF_TWO = 2.0 * RHO_ONE / 0.9
ROOT = COEF_TWO**0.5

LANES = 128
SUB = 8
HALVES = 2
DEPTH = HALVES * LANES
HALO = 8
PLANES = 64
ROWS = 32
STEPS = 4
REACH = 10
PART = 16
MIDDLE = PLANES - 2 * PART
PREPARED = 4
PACK_BYTES = 50 * 2**20
WINDOW_BYTES = 40 * 2**20


def rotated_sum(low, high, first_lane, last_lane):
    right_low = pltpu.roll(low, 1, 1)
    right_high = pltpu.roll(high, 1, 1)
    left_low = pltpu.roll(low, LANES - 1, 1)
    left_high = pltpu.roll(high, LANES - 1, 1)
    return (
        jnp.where(first_lane, 0.0, right_low) + jnp.where(last_lane, left_high, left_low),
        jnp.where(first_lane, right_low, right_high) + jnp.where(last_lane, 0.0, left_high),
    )


def place(tiles, cell, shift=0):
    return cell % HALVES, pl.ds(SUB + cell // HALVES + shift, SUB, stride=tiles), slice(None)


def sweep(tiles, rotated, planes, group_planes, field, band, depth, emit, finish=None):
    others = tiles - rotated
    size = group_planes * others * SUB

    def load(plane, cell, shift=0):
        return field[(plane, *place(tiles, cell, shift))]

    def body(group, _):
        base = group * group_planes
        lane = lax.broadcasted_iota(jnp.int32, (SUB, LANES), 1)
        first_lane = lane == 0
        last_lane = lane == LANES - 1
        block = jnp.concatenate([
            jnp.concatenate([load(base + 1 + plane, 2 * tile), load(base + 1 + plane, 2 * tile + 1)], axis=1)
            for plane in range(group_planes)
            for tile in range(rotated, tiles)
        ])
        coarse = block.astype(jnp.bfloat16)
        fine = (block - coarse.astype(jnp.float32)).astype(jnp.bfloat16)
        parts = jnp.concatenate([coarse, fine], axis=0)
        sums = jnp.dot(parts, band[...], preferred_element_type=jnp.float32)
        depth[...] = sums[:size] + sums[size:]
        for tile in range(tiles):
            pair = [2 * tile + half for half in range(HALVES)]
            before = [load(base, cell) for cell in pair]
            here = [load(base + 1, cell) for cell in pair]
            for plane in range(group_planes):
                at = base + plane
                after = [load(at + 2, cell) for cell in pair]
                if tile < rotated:
                    along = rotated_sum(here[0], here[1], first_lane, last_lane)
                else:
                    rows = pl.ds((plane * others + tile - rotated) * SUB, SUB)
                    along = [depth[rows, pl.ds(half * LANES, LANES)] for half in range(HALVES)]
                for half, cell in enumerate(pair):
                    beside = load(at + 1, cell, -1) + load(at + 1, cell, 1)
                    around = ((before[half] + after[half]) + beside) + along[half]
                    emit(at, cell, here[half], around)
                before, here = here, after
        if finish is not None:
            finish(group)
        return 0

    lax.fori_loop(0, planes // group_planes, body, 0)


def pack_kernel(
    widths, pressure, storage, source, sides, edge, middle, on_chip, sems,
):
    odd = lax.rem(lax.axis_index("dev"), 2)
    off_rows = pl.ds(pl.multiple_of(odd * (ROWS - HALO), SUB), HALO)
    on_rows = pl.ds(pl.multiple_of((1 - odd) * (ROWS - HALO), SUB), HALO)
    fields = (pressure, storage, source)
    everything = [(own, 0, own.shape[0]) for own in (*fields, sides)]
    ends = [(own, at, PART) for own in fields for at in (0, widths[0] - PART)]
    ends.append((sides, 0, 2 * STEPS))
    moves = []
    for out, rows, parts in (
        (edge, off_rows, ends),
        (on_chip, on_rows, everything),
        (middle, off_rows, [(own, PART, MIDDLE) for own in fields]),
    ):
        at = 0
        for own, start, count in parts:
            move = pltpu.make_async_copy(
                own.at[pl.ds(start, count), rows, :], out.at[pl.ds(at, count)], sems.at[len(moves)]
            )
            move.start()
            moves.append(move)
            at += count
    for move in moves:
        move.wait()


def window_kernel(kind, tiles, rotated, group_planes, own_rows, widths, *refs):
    refs = iter(refs)

    def take(count):
        return [next(refs) for _ in range(count)]

    fields = take(3)
    sides = take(1)[0]
    halos = take(2 if kind == "outer" else 1)
    with_field, with_traces = kind != "corner", kind != "outer"
    take({"inner": 0, "corner": 2, "outer": 2}[kind])
    field_out = take(1)[0] if with_field else None
    trace_outs = take(2) if with_traces else []
    naturals = take(2)
    side_naturals = take(2)
    trace_nats = take(2) if with_traces else []
    u_even, u_odd, change, f, inverse, band, depth, in_sems, out_sems = take(9)

    cells = tiles * HALVES
    planes = 2 * REACH if kind == "corner" else PLANES
    kept_rows = ROWS - HALO if kind == "inner" else HALO
    true_width = widths[0]
    width = planes if kind == "corner" else true_width
    odd = lax.rem(lax.axis_index("dev"), 2)
    at_end = 1 - odd if kind == "inner" else odd
    own_src = pl.ds(pl.multiple_of(at_end * (ROWS - own_rows), SUB), own_rows)
    own_dst = pl.ds(pl.multiple_of((1 - at_end) * HALO, SUB), own_rows)
    halo_dst = pl.ds(pl.multiple_of(at_end * own_rows, SUB), HALO)
    kept_src = pl.ds(HALO, kept_rows)
    kept_dst = pl.ds(pl.multiple_of(at_end * (ROWS - kept_rows), SUB), kept_rows)

    used = 0

    def fetch(src, src_start, src_rows, dst, dst_start, dst_rows, count):
        nonlocal used
        copies = []
        if dst is u_even:
            dst_start = 1 + dst_start
            dst_rows = pl.ds(SUB + dst_rows.start, dst_rows.size)
        for half in range(HALVES):
            copy = pltpu.make_async_copy(
                src.at[pl.ds(src_start, count), src_rows, pl.ds(half * LANES, LANES)],
                dst.at[pl.ds(dst_start, count), half, dst_rows, :],
                in_sems.at[used],
            )
            copy.start()
            copies.append(copy)
            used += 1
        return copies

    whole = pl.ds(0, HALO)
    loaded = (u_even, *naturals)
    bounds = (0, planes) if kind == "corner" else (0, PART, planes)
    chunks = len(bounds) - 1
    waits = [[] for _ in range(chunks)]
    late = []
    for chunk in range(chunks):
        at, size = bounds[chunk], bounds[chunk + 1] - bounds[chunk]
        for index, (own, nat) in enumerate(zip(fields, loaded)):
            if kind == "corner":
                waits[0] += fetch(own, 0, own_src, nat, 0, own_dst, REACH)
                waits[0] += fetch(own, true_width - REACH, own_src, nat, REACH, own_dst, REACH)
                low, high = 2 * index * PART, 2 * (index + 1) * PART - REACH
                waits[0] += fetch(halos[0], low, whole, nat, 0, halo_dst, REACH)
                waits[0] += fetch(halos[0], high, whole, nat, REACH, halo_dst, REACH)
            else:
                waits[chunk] += fetch(own, at, own_src, nat, at, own_dst, size)
                if kind == "inner":
                    waits[chunk] += fetch(halos[0], index * planes + at, whole, nat, at, halo_dst, size)
                elif chunk == 0:
                    waits[0] += fetch(halos[0], 2 * index * PART, whole, nat, 0, halo_dst, PART)
                    waits[0] += fetch(halos[1], index * MIDDLE, whole, nat, PART, halo_dst, MIDDLE)
    side_waits = []
    side_at = 3 * (PLANES if kind == "inner" else 2 * PART)
    for index, nat in enumerate(side_naturals):
        side_waits += fetch(sides, index * STEPS, own_src, nat, 0, own_dst, STEPS)
        side_waits += fetch(halos[0], side_at + index * STEPS, whole, nat, 0, halo_dst, STEPS)

    row_at = lax.broadcasted_iota(jnp.int32, (DEPTH, DEPTH), 0)
    column_at = lax.broadcasted_iota(jnp.int32, (DEPTH, DEPTH), 1)
    band[...] = jnp.where(jnp.abs(row_at - column_at) == 1, 1.0, 0.0).astype(jnp.bfloat16)
    for plane in (0, planes + 1):
        for field in (u_even, u_odd, change):
            field[plane] = jnp.zeros(field.shape[1:], jnp.float32)

    def strided(tile):
        return pl.ds(tile, SUB, stride=tiles)

    def own_part(x):
        return 4.0 + jnp.where(x == 0, BETA, 1.0) + jnp.where(x == width - 1, BETA, 1.0)

    def prepare(index, _):
        for plane in range(PREPARED):
            x = index * PREPARED + plane
            for cell in range(cells):
                half, rows = cell % 2, strided(cell // 2)
                coef, rate = (nat[x, half, rows, :] for nat in naturals)
                live = jnp.full((SUB, LANES), x, jnp.int32) < width
                f[x, cell] = jnp.where(live, rate, 0.0)
                inside = jnp.logical_and(live, coef > 0.0)
                inverse[x, cell] = jnp.where(inside, ROOT / (coef + own_part(x)), 0.0)
        return 0

    for chunk in range(chunks):
        for copy in waits[chunk] + late:
            copy.wait()
        late = []
        if kind == "outer" and chunk == 0:
            for index, nat in enumerate(loaded):
                late += fetch(
                    halos[0], (2 * index + 1) * PART, whole, nat, true_width - PART, halo_dst, PART
                )
        lax.fori_loop(bounds[chunk] // PREPARED, bounds[chunk + 1] // PREPARED, prepare, 0)
    for copy in side_waits:
        copy.wait()

    def clear(x, _):
        u_even[x + 1] = jnp.zeros(u_even.shape[1:], jnp.float32)
        return 0

    if kind != "corner":
        lax.fori_loop(width, planes, clear, 0)

    def field_copies(index):
        part = pl.ds(index * group_planes, group_planes)
        held = pl.ds(1 + index * group_planes, group_planes)
        return [
            pltpu.make_async_copy(
                u_even.at[held, half, pl.ds(SUB + HALO, kept_rows), :],
                field_out.at[part, kept_dst, pl.ds(half * LANES, LANES)],
                out_sems.at[4 + 2 * index + half],
            )
            for half in range(HALVES)
        ]

    def put_field(index):
        for copy in field_copies(index):
            copy.start()

    def advance(step, u, u_next):
        for cell in range(cells):
            half, rows = cell % 2, strided(cell // 2)
            for x, side in ((0, side_naturals[0]), (width - 1, side_naturals[1])):
                f[x, cell] = naturals[1][x, half, rows, :] + side[step, half, rows, :]

        def first_half(x, cell, here, around):
            rest = (f[x, cell] - own_part(x) * here) + around
            change[(x + 1, *place(tiles, cell))] = rest * inverse[x, cell]

        def second_half(x, cell, here, around):
            value = (u[(x + 1, *place(tiles, cell))] + ROOT * here) + around * inverse[x, cell]
            u_next[(x + 1, *place(tiles, cell))] = value

        def finish(index):
            if with_field and u is u_odd:
                pl.when(step == STEPS - 1)(lambda: put_field(index))

        sweep(tiles, rotated, planes, group_planes, u, band, depth, first_half)
        sweep(tiles, rotated, planes, group_planes, change, band, depth, second_half, finish)
        if not with_traces:
            return
        for cell in range(cells):
            half, rows = cell % 2, strided(cell // 2)
            for nat, end, inward in ((trace_nats[0], width, width - 1), (trace_nats[1], 1, 2)):
                at_end_plane = u_next[(end, *place(tiles, cell))]
                nat[step, half, rows, :] = BETA * at_end_plane + (
                    at_end_plane - u_next[(inward, *place(tiles, cell))]
                )

    def two_steps(index, _):
        advance(2 * index, u_even, u_odd)
        advance(2 * index + 1, u_odd, u_even)
        return 0

    lax.fori_loop(0, STEPS // 2, two_steps, 0)

    copies = []
    for nat, out in zip(trace_nats, trace_outs):
        for half in range(HALVES):
            copy = pltpu.make_async_copy(
                nat.at[:, half, kept_src, :],
                out.at[:, kept_dst, pl.ds(half * LANES, LANES)],
                out_sems.at[len(copies)],
            )
            copy.start()
            copies.append(copy)
    if with_field:
        for index in range(planes // group_planes):
            copies += field_copies(index)
    for copy in copies:
        copy.wait()


ANYWHERE = pl.BlockSpec(memory_space=pl.ANY)
IN_HBM = pl.BlockSpec(memory_space=pltpu.HBM)
IN_SMEM = pl.BlockSpec(memory_space=pltpu.SMEM)


def run_window(kind, tiles, rotated, group_planes, limit, args, halos, previous=(), after=()):
    planes = 2 * REACH if kind == "corner" else PLANES
    rows = tiles * SUB
    cells = tiles * HALVES
    natural = pltpu.VMEM((planes, HALVES, rows, LANES), jnp.float32)
    narrow = pltpu.VMEM((STEPS, HALVES, rows, LANES), jnp.float32)
    tiled = pltpu.VMEM((planes, cells, SUB, LANES), jnp.float32)
    padded = pltpu.VMEM((planes + 2, HALVES, rows + 2 * SUB, LANES), jnp.float32)
    field = jax.ShapeDtypeStruct(args[1].shape, jnp.float32)
    trace = jax.ShapeDtypeStruct((STEPS, ROWS, DEPTH), jnp.float32)
    outs = {"inner": (field, trace, trace), "corner": (trace, trace), "outer": (field,)}[kind]
    return pl.pallas_call(
        functools.partial(window_kernel, kind, tiles, rotated, group_planes, rows - HALO),
        out_shape=outs,
        in_specs=[IN_SMEM] + [IN_HBM] * 3 + [ANYWHERE] * len((args[4], *halos, *previous, *after)),
        out_specs=(ANYWHERE,) * len(outs),
        input_output_aliases={5 + len(halos) + i: i for i in range(len(previous))},
        scratch_shapes=[
            *[natural] * 2, *[narrow] * 2,
            *([] if kind == "outer" else [narrow] * 2),
            padded, padded, padded, tiled, tiled,
            pltpu.VMEM((DEPTH, DEPTH), jnp.bfloat16),
            pltpu.VMEM((group_planes * (tiles - rotated) * SUB, DEPTH), jnp.float32),
            pltpu.SemaphoreType.DMA((64,)),
            pltpu.SemaphoreType.DMA((4 + HALVES * planes // group_planes,)),
        ],
        compiler_params=pltpu.CompilerParams(vmem_limit_bytes=limit),
        cost_estimate=pl.CostEstimate(
            flops=planes * rows * DEPTH * 22 * STEPS,
            bytes_accessed=4 * planes * rows * DEPTH * 4,
            transcendentals=0,
        ),
        name=kind,
    )(*args, *halos, *previous, *after)


def on_device(pressure, storage, source, left_data, right_data, widths):
    sides = jnp.concatenate([left_data[0], right_data[0]])
    args = (widths, pressure, storage, source, sides)
    rims = [
        jax.ShapeDtypeStruct((planes, HALO, DEPTH), jnp.float32)
        for planes in (6 * PART + 2 * STEPS, 3 * MIDDLE, 3 * PLANES + 2 * STEPS)
    ]
    edge, middle, on_chip = pl.pallas_call(
        pack_kernel,
        out_shape=tuple(rims),
        in_specs=[IN_SMEM] + [IN_HBM] * 3 + [ANYWHERE],
        out_specs=(ANYWHERE,) * 3,
        scratch_shapes=[pltpu.SemaphoreType.DMA((16,))],
        compiler_params=pltpu.CompilerParams(vmem_limit_bytes=PACK_BYTES),
        name="pack",
    )(*args)
    count = lax.axis_size("dev")
    chips = [(i, i + 1) for i in range(1, count - 1, 2)]
    chips += [(j, i) for i, j in chips]
    cores = [(i, i + 1) for i in range(0, count, 2)]
    cores += [(j, i) for i, j in cores]
    edge = lax.ppermute(edge, "dev", chips)
    on_chip = lax.ppermute(on_chip, "dev", cores)
    middle = lax.ppermute(middle, "dev", chips)

    field, trace_high, trace_low = run_window("inner", 5, 3, 16, WINDOW_BYTES, args, (on_chip,))
    trace_high, trace_low = run_window("corner", 3, 2, 10, WINDOW_BYTES, args, (edge,), (trace_high, trace_low))

    subs = lax.axis_size("sub")
    up = [(i, i + 1) for i in range(subs - 1)]
    down = [(i + 1, i) for i in range(subs - 1)]
    new_left = lax.ppermute(trace_high, "sub", up)
    new_right = lax.ppermute(trace_low, "sub", down)
    (field,) = run_window("outer", 3, 2, 16, WINDOW_BYTES, args, (edge, middle), (field,), (trace_low,))
    return (field, new_left[None], new_right[None])


def solution(mesh):
    in_specs = (
        P("sub", "dev", None),
        P("sub", "dev", None),
        P("sub", "dev", None),
        P("sub", None, "dev", None),
        P("sub", None, "dev", None),
        P("sub"),
    )
    out_specs = (P("sub", "dev", None), P("sub", None, "dev", None), P("sub", None, "dev", None))
    return jax.shard_map(
        on_device, mesh=mesh, in_specs=in_specs, out_specs=out_specs, check_vma=False
    )
```

```python
import functools

import jax
import jax.numpy as jnp
from jax import lax
from jax.experimental import pallas as pl
from jax.experimental.pallas import tpu as pltpu
from jax.sharding import PartitionSpec as P

BETA = 1.5
RHO_ZERO = 0.9
RHO_ONE = 1.0 / (2.0 / 0.9 - 0.9)
COEF_TWO = 2.0 * RHO_ONE / 0.9
ROOT = COEF_TWO**0.5

LANES = 128
SUB = 8
HALVES = 2
DEPTH = HALVES * LANES
HALO = 8
PLANES = 64
ROWS = 32
STEPS = 4
REACH = 10
PART = 16
MIDDLE = PLANES - 2 * PART
PREPARED = 4
PACK_BYTES = 50 * 2**20
WINDOW_BYTES = 40 * 2**20


def rotated_sum(low, high, first_lane, last_lane):
    right_low = pltpu.roll(low, 1, 1)
    right_high = pltpu.roll(high, 1, 1)
    left_low = pltpu.roll(low, LANES - 1, 1)
    left_high = pltpu.roll(high, LANES - 1, 1)
    return (
        jnp.where(first_lane, 0.0, right_low) + jnp.where(last_lane, left_high, left_low),
        jnp.where(first_lane, right_low, right_high) + jnp.where(last_lane, 0.0, left_high),
    )


def place(cell):
    return pl.ds(SUB * (cell // 2), SUB), pl.ds(LANES * (cell % 2), LANES)


def sweep(tiles, rotated, planes, group_planes, field, band, depth, emit, finish=None):
    cells = tiles * HALVES
    others = tiles - rotated
    size = group_planes * others * SUB

    def load(plane, cell):
        return field[(plane, *place(cell % cells))]

    def body(group, _):
        base = group * group_planes
        lane = lax.broadcasted_iota(jnp.int32, (SUB, LANES), 1)
        first_lane = lane == 0
        last_lane = lane == LANES - 1
        block = field[pl.ds(base + 1, group_planes), pl.ds(rotated * SUB, others * SUB), :]
        block = block.reshape(size, DEPTH)
        coarse = block.astype(jnp.bfloat16)
        fine = (block - coarse.astype(jnp.float32)).astype(jnp.bfloat16)
        parts = jnp.concatenate([coarse, fine], axis=0)
        sums = jnp.dot(parts, band[...], preferred_element_type=jnp.float32)
        depth[...] = sums[:size] + sums[size:]
        for tile in range(tiles):
            pair = [2 * tile + half for half in range(HALVES)]
            before = [load(base, cell) for cell in pair]
            here = [load(base + 1, cell) for cell in pair]
            for plane in range(group_planes):
                at = base + plane
                after = [load(at + 2, cell) for cell in pair]
                if tile < rotated:
                    along = rotated_sum(here[0], here[1], first_lane, last_lane)
                else:
                    rows = pl.ds((plane * others + tile - rotated) * SUB, SUB)
                    along = [depth[rows, pl.ds(half * LANES, LANES)] for half in range(HALVES)]
                for half, cell in enumerate(pair):
                    above = load(at + 1, cell - 2)
                    if tile == 0:
                        above = pltpu.roll(above, 1, 0)
                    below = load(at + 1, cell + 2)
                    if tile == tiles - 1:
                        below = pltpu.roll(below, SUB - 1, 0)
                    around = ((before[half] + after[half]) + (above + below)) + along[half]
                    emit(at, cell, here[half], around)
                before, here = here, after
        if finish is not None:
            finish(group)
        return 0

    lax.fori_loop(0, planes // group_planes, body, 0)


def pack_kernel(
    widths, pressure, storage, source, sides, edge, middle, on_chip, sems,
):
    odd = lax.rem(lax.axis_index("dev"), 2)
    off_rows = pl.ds(pl.multiple_of(odd * (ROWS - HALO), SUB), HALO)
    on_rows = pl.ds(pl.multiple_of((1 - odd) * (ROWS - HALO), SUB), HALO)
    fields = (pressure, storage, source)
    everything = [(own, 0, own.shape[0]) for own in (*fields, sides)]
    ends = [(own, at, PART) for own in fields for at in (0, widths[0] - PART)]
    ends.append((sides, 0, 2 * STEPS))
    moves = []
    for out, rows, parts in (
        (edge, off_rows, ends),
        (on_chip, on_rows, everything),
        (middle, off_rows, [(own, PART, MIDDLE) for own in fields]),
    ):
        at = 0
        for own, start, count in parts:
            move = pltpu.make_async_copy(
                own.at[pl.ds(start, count), rows, :], out.at[pl.ds(at, count)], sems.at[len(moves)]
            )
            move.start()
            moves.append(move)
            at += count
    for move in moves:
        move.wait()


def window_kernel(kind, tiles, rotated, group_planes, own_rows, widths, *refs):
    refs = iter(refs)

    def take(count):
        return [next(refs) for _ in range(count)]

    fields = take(3)
    sides = take(1)[0]
    halos = take(2 if kind == "outer" else 1)
    with_field, with_traces = kind != "corner", kind != "outer"
    take({"inner": 0, "corner": 2, "outer": 2}[kind])
    field_out = take(1)[0] if with_field else None
    trace_outs = take(2) if with_traces else []
    naturals = take(3)
    side_naturals = take(2)
    out_nat = take(1)[0] if with_field else None
    trace_nats = take(2) if with_traces else []
    u_even, u_odd, change, f, inverse, band, depth, in_sems, out_sems = take(9)

    cells = tiles * HALVES
    planes = 2 * REACH if kind == "corner" else PLANES
    kept_rows = ROWS - HALO if kind == "inner" else HALO
    true_width = widths[0]
    width = planes if kind == "corner" else true_width
    odd = lax.rem(lax.axis_index("dev"), 2)
    at_end = 1 - odd if kind == "inner" else odd
    own_src = pl.ds(pl.multiple_of(at_end * (ROWS - own_rows), SUB), own_rows)
    own_dst = pl.ds(pl.multiple_of((1 - at_end) * HALO, SUB), own_rows)
    halo_dst = pl.ds(pl.multiple_of(at_end * own_rows, SUB), HALO)
    kept_src = pl.ds(HALO, kept_rows)
    kept_dst = pl.ds(pl.multiple_of(at_end * (ROWS - kept_rows), SUB), kept_rows)

    used = 0

    def fetch(src, src_start, src_rows, dst, dst_start, dst_rows, count):
        nonlocal used
        copies = []
        for half in range(HALVES):
            copy = pltpu.make_async_copy(
                src.at[pl.ds(src_start, count), src_rows, pl.ds(half * LANES, LANES)],
                dst.at[pl.ds(dst_start, count), half, dst_rows, :],
                in_sems.at[used],
            )
            copy.start()
            copies.append(copy)
            used += 1
        return copies

    whole = pl.ds(0, HALO)
    bounds = (0, planes) if kind == "corner" else (0, PART, planes)
    chunks = len(bounds) - 1
    waits = [[] for _ in range(chunks)]
    late = []
    for chunk in range(chunks):
        at, size = bounds[chunk], bounds[chunk + 1] - bounds[chunk]
        for index, (own, nat) in enumerate(zip(fields, naturals)):
            if kind == "corner":
                waits[0] += fetch(own, 0, own_src, nat, 0, own_dst, REACH)
                waits[0] += fetch(own, true_width - REACH, own_src, nat, REACH, own_dst, REACH)
                low, high = 2 * index * PART, 2 * (index + 1) * PART - REACH
                waits[0] += fetch(halos[0], low, whole, nat, 0, halo_dst, REACH)
                waits[0] += fetch(halos[0], high, whole, nat, REACH, halo_dst, REACH)
            else:
                waits[chunk] += fetch(own, at, own_src, nat, at, own_dst, size)
                if kind == "inner":
                    waits[chunk] += fetch(halos[0], index * planes + at, whole, nat, at, halo_dst, size)
                elif chunk == 0:
                    waits[0] += fetch(halos[0], 2 * index * PART, whole, nat, 0, halo_dst, PART)
                    waits[0] += fetch(halos[1], index * MIDDLE, whole, nat, PART, halo_dst, MIDDLE)
    side_waits = []
    side_at = 3 * (PLANES if kind == "inner" else 2 * PART)
    for index, nat in enumerate(side_naturals):
        side_waits += fetch(sides, index * STEPS, own_src, nat, 0, own_dst, STEPS)
        side_waits += fetch(halos[0], side_at + index * STEPS, whole, nat, 0, halo_dst, STEPS)

    row_at = lax.broadcasted_iota(jnp.int32, (DEPTH, DEPTH), 0)
    column_at = lax.broadcasted_iota(jnp.int32, (DEPTH, DEPTH), 1)
    band[...] = jnp.where(jnp.abs(row_at - column_at) == 1, 1.0, 0.0).astype(jnp.bfloat16)
    for plane in (0, planes + 1):
        for field in (u_even, u_odd, change):
            field[plane] = jnp.zeros((tiles * SUB, DEPTH), jnp.float32)

    def strided(tile):
        return pl.ds(tile, SUB, stride=tiles)

    def own_part(x):
        return 4.0 + jnp.where(x == 0, BETA, 1.0) + jnp.where(x == width - 1, BETA, 1.0)

    def prepare(index, _):
        for plane in range(PREPARED):
            x = index * PREPARED + plane
            for cell in range(cells):
                half, rows = cell % 2, strided(cell // 2)
                first, coef, rate = (nat[x, half, rows, :] for nat in naturals)
                live = jnp.full((SUB, LANES), x, jnp.int32) < width
                u_even[(x + 1, *place(cell))] = jnp.where(live, first, 0.0)
                f[x, cell] = jnp.where(live, rate, 0.0)
                inside = jnp.logical_and(live, coef > 0.0)
                inverse[x, cell] = jnp.where(inside, ROOT / (coef + own_part(x)), 0.0)
        return 0

    for chunk in range(chunks):
        for copy in waits[chunk] + late:
            copy.wait()
        late = []
        if kind == "outer" and chunk == 0:
            for index, nat in enumerate(naturals):
                late += fetch(
                    halos[0], (2 * index + 1) * PART, whole, nat, true_width - PART, halo_dst, PART
                )
        lax.fori_loop(bounds[chunk] // PREPARED, bounds[chunk + 1] // PREPARED, prepare, 0)
    for copy in side_waits:
        copy.wait()

    def field_copies(index):
        part = pl.ds(index * group_planes, group_planes)
        return [
            pltpu.make_async_copy(
                out_nat.at[part, half, kept_src, :],
                field_out.at[part, kept_dst, pl.ds(half * LANES, LANES)],
                out_sems.at[4 + 2 * index + half],
            )
            for half in range(HALVES)
        ]

    def put_field(index):
        for copy in field_copies(index):
            copy.start()

    def advance(step, u, u_next):
        for cell in range(cells):
            half, rows = cell % 2, strided(cell // 2)
            for x, side in ((0, side_naturals[0]), (width - 1, side_naturals[1])):
                f[x, cell] = naturals[2][x, half, rows, :] + side[step, half, rows, :]

        def first_half(x, cell, here, around):
            rest = (f[x, cell] - own_part(x) * here) + around
            change[(x + 1, *place(cell))] = rest * inverse[x, cell]

        def second_half(x, cell, here, around):
            value = (u[(x + 1, *place(cell))] + ROOT * here) + around * inverse[x, cell]
            u_next[(x + 1, *place(cell))] = value
            if with_field and u is u_odd:
                out_nat[x, cell % 2, strided(cell // 2), :] = value

        def finish(index):
            if with_field and u is u_odd:
                pl.when(step == STEPS - 1)(lambda: put_field(index))

        sweep(tiles, rotated, planes, group_planes, u, band, depth, first_half)
        sweep(tiles, rotated, planes, group_planes, change, band, depth, second_half, finish)
        if not with_traces:
            return
        for cell in range(cells):
            half, rows = cell % 2, strided(cell // 2)
            for nat, end, inward in ((trace_nats[0], width, width - 1), (trace_nats[1], 1, 2)):
                at_end_plane = u_next[(end, *place(cell))]
                nat[step, half, rows, :] = BETA * at_end_plane + (
                    at_end_plane - u_next[(inward, *place(cell))]
                )

    def two_steps(index, _):
        advance(2 * index, u_even, u_odd)
        advance(2 * index + 1, u_odd, u_even)
        return 0

    lax.fori_loop(0, STEPS // 2, two_steps, 0)

    copies = []
    for nat, out in zip(trace_nats, trace_outs):
        for half in range(HALVES):
            copy = pltpu.make_async_copy(
                nat.at[:, half, kept_src, :],
                out.at[:, kept_dst, pl.ds(half * LANES, LANES)],
                out_sems.at[len(copies)],
            )
            copy.start()
            copies.append(copy)
    if with_field:
        for index in range(planes // group_planes):
            copies += field_copies(index)
    for copy in copies:
        copy.wait()


ANYWHERE = pl.BlockSpec(memory_space=pl.ANY)
IN_HBM = pl.BlockSpec(memory_space=pltpu.HBM)
IN_SMEM = pl.BlockSpec(memory_space=pltpu.SMEM)


def run_window(kind, tiles, rotated, group_planes, limit, args, halos, previous=(), after=()):
    planes = 2 * REACH if kind == "corner" else PLANES
    rows = tiles * SUB
    cells = tiles * HALVES
    natural = pltpu.VMEM((planes, HALVES, rows, LANES), jnp.float32)
    narrow = pltpu.VMEM((STEPS, HALVES, rows, LANES), jnp.float32)
    tiled = pltpu.VMEM((planes, cells, SUB, LANES), jnp.float32)
    padded = pltpu.VMEM((planes + 2, rows, DEPTH), jnp.float32)
    field = jax.ShapeDtypeStruct(args[1].shape, jnp.float32)
    trace = jax.ShapeDtypeStruct((STEPS, ROWS, DEPTH), jnp.float32)
    outs = {"inner": (field, trace, trace), "corner": (trace, trace), "outer": (field,)}[kind]
    return pl.pallas_call(
        functools.partial(window_kernel, kind, tiles, rotated, group_planes, rows - HALO),
        out_shape=outs,
        in_specs=[IN_SMEM] + [IN_HBM] * 3 + [ANYWHERE] * len((args[4], *halos, *previous, *after)),
        out_specs=(ANYWHERE,) * len(outs),
        input_output_aliases={5 + len(halos) + i: i for i in range(len(previous))},
        scratch_shapes=[
            *[natural] * 3, *[narrow] * 2,
            *([] if kind == "corner" else [natural]), *([] if kind == "outer" else [narrow] * 2),
            padded, padded, padded, tiled, tiled,
            pltpu.VMEM((DEPTH, DEPTH), jnp.bfloat16),
            pltpu.VMEM((group_planes * (tiles - rotated) * SUB, DEPTH), jnp.float32),
            pltpu.SemaphoreType.DMA((64,)),
            pltpu.SemaphoreType.DMA((4 + HALVES * planes // group_planes,)),
        ],
        compiler_params=pltpu.CompilerParams(vmem_limit_bytes=limit),
        cost_estimate=pl.CostEstimate(
            flops=planes * rows * DEPTH * 22 * STEPS,
            bytes_accessed=4 * planes * rows * DEPTH * 4,
            transcendentals=0,
        ),
        name=kind,
    )(*args, *halos, *previous, *after)


def on_device(pressure, storage, source, left_data, right_data, widths):
    sides = jnp.concatenate([left_data[0], right_data[0]])
    args = (widths, pressure, storage, source, sides)
    rims = [
        jax.ShapeDtypeStruct((planes, HALO, DEPTH), jnp.float32)
        for planes in (6 * PART + 2 * STEPS, 3 * MIDDLE, 3 * PLANES + 2 * STEPS)
    ]
    edge, middle, on_chip = pl.pallas_call(
        pack_kernel,
        out_shape=tuple(rims),
        in_specs=[IN_SMEM] + [IN_HBM] * 3 + [ANYWHERE],
        out_specs=(ANYWHERE,) * 3,
        scratch_shapes=[pltpu.SemaphoreType.DMA((16,))],
        compiler_params=pltpu.CompilerParams(vmem_limit_bytes=PACK_BYTES),
        name="pack",
    )(*args)
    count = lax.axis_size("dev")
    chips = [(i, i + 1) for i in range(1, count - 1, 2)]
    chips += [(j, i) for i, j in chips]
    cores = [(i, i + 1) for i in range(0, count, 2)]
    cores += [(j, i) for i, j in cores]
    edge = lax.ppermute(edge, "dev", chips)
    on_chip = lax.ppermute(on_chip, "dev", cores)
    middle = lax.ppermute(middle, "dev", chips)

    field, trace_high, trace_low = run_window("inner", 5, 4, 32, WINDOW_BYTES, args, (on_chip,))
    trace_high, trace_low = run_window("corner", 3, 2, 20, WINDOW_BYTES, args, (edge,), (trace_high, trace_low))

    subs = lax.axis_size("sub")
    up = [(i, i + 1) for i in range(subs - 1)]
    down = [(i + 1, i) for i in range(subs - 1)]
    new_left = lax.ppermute(trace_high, "sub", up)
    new_right = lax.ppermute(trace_low, "sub", down)
    (field,) = run_window("outer", 3, 2, 32, WINDOW_BYTES, args, (edge, middle), (field,), (trace_low,))
    return (field, new_left[None], new_right[None])


def solution(mesh):
    in_specs = (
        P("sub", "dev", None),
        P("sub", "dev", None),
        P("sub", "dev", None),
        P("sub", None, "dev", None),
        P("sub", None, "dev", None),
        P("sub"),
    )
    out_specs = (P("sub", "dev", None), P("sub", None, "dev", None), P("sub", None, "dev", None))
    return jax.shard_map(
        on_device, mesh=mesh, in_specs=in_specs, out_specs=out_specs, check_vma=False
    )
```

```python
import functools

import jax
import jax.numpy as jnp
from jax import lax
from jax.experimental import pallas as pl
from jax.experimental.pallas import tpu as pltpu
from jax.sharding import PartitionSpec as P

BETA = 1.5
RHO_ZERO = 0.9
RHO_ONE = 1.0 / (2.0 / 0.9 - 0.9)
COEF_TWO = 2.0 * RHO_ONE / 0.9
ROOT = COEF_TWO**0.5

LANES = 128
SUB = 8
HALVES = 2
DEPTH = HALVES * LANES
HALO = 8
PLANES = 64
ROWS = 32
STEPS = 4
REACH = 10
PART = 16
MIDDLE = PLANES - 2 * PART
PREPARED = 4
PACK_BYTES = 50 * 2**20
WINDOW_BYTES = 40 * 2**20


def rotated_sum(low, high, first_lane, last_lane):
    right_low = pltpu.roll(low, 1, 1)
    right_high = pltpu.roll(high, 1, 1)
    left_low = pltpu.roll(low, LANES - 1, 1)
    left_high = pltpu.roll(high, LANES - 1, 1)
    return (
        jnp.where(first_lane, 0.0, right_low) + jnp.where(last_lane, left_high, left_low),
        jnp.where(first_lane, right_low, right_high) + jnp.where(last_lane, 0.0, left_high),
    )


def place(cell):
    return pl.ds(SUB * (cell // 2), SUB), pl.ds(LANES * (cell % 2), LANES)


def sweep(tiles, rotated, planes, group_planes, field, band, depth, emit, finish=None):
    cells = tiles * HALVES
    others = tiles - rotated
    size = group_planes * others * SUB

    def load(plane, cell):
        return field[(plane, *place(cell % cells))]

    def body(group, _):
        base = group * group_planes
        lane = lax.broadcasted_iota(jnp.int32, (SUB, LANES), 1)
        first_lane = lane == 0
        last_lane = lane == LANES - 1
        block = field[pl.ds(base + 1, group_planes), pl.ds(rotated * SUB, others * SUB), :]
        block = block.reshape(size, DEPTH)
        coarse = block.astype(jnp.bfloat16)
        fine = (block - coarse.astype(jnp.float32)).astype(jnp.bfloat16)
        parts = jnp.concatenate([coarse, fine], axis=0)
        sums = jnp.dot(parts, band[...], preferred_element_type=jnp.float32)
        depth[...] = sums[:size] + sums[size:]
        for tile in range(tiles):
            pair = [2 * tile + half for half in range(HALVES)]
            before = [load(base, cell) for cell in pair]
            here = [load(base + 1, cell) for cell in pair]
            for plane in range(group_planes):
                at = base + plane
                after = [load(at + 2, cell) for cell in pair]
                if tile < rotated:
                    along = rotated_sum(here[0], here[1], first_lane, last_lane)
                else:
                    rows = pl.ds((plane * others + tile - rotated) * SUB, SUB)
                    along = [depth[rows, pl.ds(half * LANES, LANES)] for half in range(HALVES)]
                for half, cell in enumerate(pair):
                    above = load(at + 1, cell - 2)
                    if tile == 0:
                        above = pltpu.roll(above, 1, 0)
                    below = load(at + 1, cell + 2)
                    if tile == tiles - 1:
                        below = pltpu.roll(below, SUB - 1, 0)
                    around = ((before[half] + after[half]) + (above + below)) + along[half]
                    emit(at, cell, here[half], around)
                before, here = here, after
        if finish is not None:
            finish(group)
        return 0

    lax.fori_loop(0, planes // group_planes, body, 0)


def pack_kernel(
    widths, pressure, storage, source, sides, edge, middle, on_chip, sems,
):
    odd = lax.rem(lax.axis_index("dev"), 2)
    off_rows = pl.ds(pl.multiple_of(odd * (ROWS - HALO), SUB), HALO)
    on_rows = pl.ds(pl.multiple_of((1 - odd) * (ROWS - HALO), SUB), HALO)
    fields = (pressure, storage, source)
    everything = [(own, 0, own.shape[0]) for own in (*fields, sides)]
    ends = [(own, at, PART) for own in fields for at in (0, widths[0] - PART)]
    ends.append((sides, 0, 2 * STEPS))
    moves = []
    for out, rows, parts in (
        (edge, off_rows, ends),
        (on_chip, on_rows, everything),
        (middle, off_rows, [(own, PART, MIDDLE) for own in fields]),
    ):
        at = 0
        for own, start, count in parts:
            move = pltpu.make_async_copy(
                own.at[pl.ds(start, count), rows, :], out.at[pl.ds(at, count)], sems.at[len(moves)]
            )
            move.start()
            moves.append(move)
            at += count
    for move in moves:
        move.wait()


def window_kernel(kind, tiles, rotated, group_planes, own_rows, widths, *refs):
    refs = iter(refs)

    def take(count):
        return [next(refs) for _ in range(count)]

    fields = take(3)
    sides = take(1)[0]
    halos = take(2 if kind == "outer" else 1)
    with_field, with_traces = kind != "corner", kind != "outer"
    take({"inner": 0, "corner": 2, "outer": 2}[kind])
    field_out = take(1)[0] if with_field else None
    trace_outs = take(2) if with_traces else []
    naturals = take(3)
    side_naturals = take(2)
    out_nat = take(1)[0] if with_field else None
    trace_nats = take(2) if with_traces else []
    u_even, u_odd, change, f, inverse, band, depth, in_sems, out_sems = take(9)

    cells = tiles * HALVES
    planes = 2 * REACH if kind == "corner" else PLANES
    kept_rows = ROWS - HALO if kind == "inner" else HALO
    true_width = widths[0]
    width = planes if kind == "corner" else true_width
    odd = lax.rem(lax.axis_index("dev"), 2)
    at_end = 1 - odd if kind == "inner" else odd
    own_src = pl.ds(pl.multiple_of(at_end * (ROWS - own_rows), SUB), own_rows)
    own_dst = pl.ds(pl.multiple_of((1 - at_end) * HALO, SUB), own_rows)
    halo_dst = pl.ds(pl.multiple_of(at_end * own_rows, SUB), HALO)
    kept_src = pl.ds(HALO, kept_rows)
    kept_dst = pl.ds(pl.multiple_of(at_end * (ROWS - kept_rows), SUB), kept_rows)

    used = 0

    def fetch(src, src_start, src_rows, dst, dst_start, dst_rows, count):
        nonlocal used
        copies = []
        for half in range(HALVES):
            copy = pltpu.make_async_copy(
                src.at[pl.ds(src_start, count), src_rows, pl.ds(half * LANES, LANES)],
                dst.at[pl.ds(dst_start, count), half, dst_rows, :],
                in_sems.at[used],
            )
            copy.start()
            copies.append(copy)
            used += 1
        return copies

    whole = pl.ds(0, HALO)
    bounds = (0, planes) if kind == "corner" else (0, PART, planes)
    chunks = len(bounds) - 1
    waits = [[] for _ in range(chunks)]
    late = []
    for chunk in range(chunks):
        at, size = bounds[chunk], bounds[chunk + 1] - bounds[chunk]
        for index, (own, nat) in enumerate(zip(fields, naturals)):
            if kind == "corner":
                waits[0] += fetch(own, 0, own_src, nat, 0, own_dst, REACH)
                waits[0] += fetch(own, true_width - REACH, own_src, nat, REACH, own_dst, REACH)
                low, high = 2 * index * PART, 2 * (index + 1) * PART - REACH
                waits[0] += fetch(halos[0], low, whole, nat, 0, halo_dst, REACH)
                waits[0] += fetch(halos[0], high, whole, nat, REACH, halo_dst, REACH)
            else:
                waits[chunk] += fetch(own, at, own_src, nat, at, own_dst, size)
                if kind == "inner":
                    waits[chunk] += fetch(halos[0], index * planes + at, whole, nat, at, halo_dst, size)
                elif chunk == 0:
                    waits[0] += fetch(halos[0], 2 * index * PART, whole, nat, 0, halo_dst, PART)
                    waits[0] += fetch(halos[1], index * MIDDLE, whole, nat, PART, halo_dst, MIDDLE)
    side_waits = []
    side_at = 3 * (PLANES if kind == "inner" else 2 * PART)
    for index, nat in enumerate(side_naturals):
        side_waits += fetch(sides, index * STEPS, own_src, nat, 0, own_dst, STEPS)
        side_waits += fetch(halos[0], side_at + index * STEPS, whole, nat, 0, halo_dst, STEPS)

    row_at = lax.broadcasted_iota(jnp.int32, (DEPTH, DEPTH), 0)
    column_at = lax.broadcasted_iota(jnp.int32, (DEPTH, DEPTH), 1)
    band[...] = jnp.where(jnp.abs(row_at - column_at) == 1, 1.0, 0.0).astype(jnp.bfloat16)
    for plane in (0, planes + 1):
        for field in (u_even, u_odd, change):
            field[plane] = jnp.zeros((tiles * SUB, DEPTH), jnp.float32)

    def strided(tile):
        return pl.ds(tile, SUB, stride=tiles)

    def own_part(x):
        return 4.0 + jnp.where(x == 0, BETA, 1.0) + jnp.where(x == width - 1, BETA, 1.0)

    def prepare(index, _):
        for plane in range(PREPARED):
            x = index * PREPARED + plane
            for cell in range(cells):
                half, rows = cell % 2, strided(cell // 2)
                first, coef, rate = (nat[x, half, rows, :] for nat in naturals)
                live = jnp.full((SUB, LANES), x, jnp.int32) < width
                u_even[(x + 1, *place(cell))] = jnp.where(live, first, 0.0)
                f[x, cell] = jnp.where(live, rate, 0.0)
                inside = jnp.logical_and(live, coef > 0.0)
                inverse[x, cell] = jnp.where(inside, ROOT / (coef + own_part(x)), 0.0)
        return 0

    for chunk in range(chunks):
        for copy in waits[chunk] + late:
            copy.wait()
        late = []
        if kind == "outer" and chunk == 0:
            for index, nat in enumerate(naturals):
                late += fetch(
                    halos[0], (2 * index + 1) * PART, whole, nat, true_width - PART, halo_dst, PART
                )
        lax.fori_loop(bounds[chunk] // PREPARED, bounds[chunk + 1] // PREPARED, prepare, 0)
    for copy in side_waits:
        copy.wait()

    def field_copies(index):
        part = pl.ds(index * group_planes, group_planes)
        return [
            pltpu.make_async_copy(
                out_nat.at[part, half, kept_src, :],
                field_out.at[part, kept_dst, pl.ds(half * LANES, LANES)],
                out_sems.at[4 + 2 * index + half],
            )
            for half in range(HALVES)
        ]

    def put_field(index):
        for copy in field_copies(index):
            copy.start()

    def advance(step, u, u_next):
        for cell in range(cells):
            half, rows = cell % 2, strided(cell // 2)
            for x, side in ((0, side_naturals[0]), (width - 1, side_naturals[1])):
                f[x, cell] = naturals[2][x, half, rows, :] + side[step, half, rows, :]

        def first_half(x, cell, here, around):
            rest = (f[x, cell] - own_part(x) * here) + around
            change[(x + 1, *place(cell))] = rest * inverse[x, cell]

        def second_half(x, cell, here, around):
            value = (u[(x + 1, *place(cell))] + ROOT * here) + around * inverse[x, cell]
            u_next[(x + 1, *place(cell))] = value
            if with_field and u is u_odd:
                out_nat[x, cell % 2, strided(cell // 2), :] = value

        def finish(index):
            if with_field and u is u_odd:
                pl.when(step == STEPS - 1)(lambda: put_field(index))

        sweep(tiles, rotated, planes, group_planes, u, band, depth, first_half)
        sweep(tiles, rotated, planes, group_planes, change, band, depth, second_half, finish)
        if not with_traces:
            return
        for cell in range(cells):
            half, rows = cell % 2, strided(cell // 2)
            for nat, end, inward in ((trace_nats[0], width, width - 1), (trace_nats[1], 1, 2)):
                at_end_plane = u_next[(end, *place(cell))]
                nat[step, half, rows, :] = BETA * at_end_plane + (
                    at_end_plane - u_next[(inward, *place(cell))]
                )

    def two_steps(index, _):
        advance(2 * index, u_even, u_odd)
        advance(2 * index + 1, u_odd, u_even)
        return 0

    lax.fori_loop(0, STEPS // 2, two_steps, 0)

    copies = []
    for nat, out in zip(trace_nats, trace_outs):
        for half in range(HALVES):
            copy = pltpu.make_async_copy(
                nat.at[:, half, kept_src, :],
                out.at[:, kept_dst, pl.ds(half * LANES, LANES)],
                out_sems.at[len(copies)],
            )
            copy.start()
            copies.append(copy)
    if with_field:
        for index in range(planes // group_planes):
            copies += field_copies(index)
    for copy in copies:
        copy.wait()


ANYWHERE = pl.BlockSpec(memory_space=pl.ANY)
IN_HBM = pl.BlockSpec(memory_space=pltpu.HBM)
IN_SMEM = pl.BlockSpec(memory_space=pltpu.SMEM)


def run_window(kind, tiles, rotated, group_planes, limit, args, halos, previous=(), after=()):
    planes = 2 * REACH if kind == "corner" else PLANES
    rows = tiles * SUB
    cells = tiles * HALVES
    natural = pltpu.VMEM((planes, HALVES, rows, LANES), jnp.float32)
    narrow = pltpu.VMEM((STEPS, HALVES, rows, LANES), jnp.float32)
    tiled = pltpu.VMEM((planes, cells, SUB, LANES), jnp.float32)
    padded = pltpu.VMEM((planes + 2, rows, DEPTH), jnp.float32)
    field = jax.ShapeDtypeStruct(args[1].shape, jnp.float32)
    trace = jax.ShapeDtypeStruct((STEPS, ROWS, DEPTH), jnp.float32)
    outs = {"inner": (field, trace, trace), "corner": (trace, trace), "outer": (field,)}[kind]
    return pl.pallas_call(
        functools.partial(window_kernel, kind, tiles, rotated, group_planes, rows - HALO),
        out_shape=outs,
        in_specs=[IN_SMEM] + [IN_HBM] * 3 + [ANYWHERE] * len((args[4], *halos, *previous, *after)),
        out_specs=(ANYWHERE,) * len(outs),
        input_output_aliases={5 + len(halos) + i: i for i in range(len(previous))},
        scratch_shapes=[
            *[natural] * 3, *[narrow] * 2,
            *([] if kind == "corner" else [natural]), *([] if kind == "outer" else [narrow] * 2),
            padded, padded, padded, tiled, tiled,
            pltpu.VMEM((DEPTH, DEPTH), jnp.bfloat16),
            pltpu.VMEM((group_planes * (tiles - rotated) * SUB, DEPTH), jnp.float32),
            pltpu.SemaphoreType.DMA((64,)),
            pltpu.SemaphoreType.DMA((4 + HALVES * planes // group_planes,)),
        ],
        compiler_params=pltpu.CompilerParams(vmem_limit_bytes=limit),
        cost_estimate=pl.CostEstimate(
            flops=planes * rows * DEPTH * 22 * STEPS,
            bytes_accessed=4 * planes * rows * DEPTH * 4,
            transcendentals=0,
        ),
        name=kind,
    )(*args, *halos, *previous, *after)


def on_device(pressure, storage, source, left_data, right_data, widths):
    sides = jnp.concatenate([left_data[0], right_data[0]])
    args = (widths, pressure, storage, source, sides)
    rims = [
        jax.ShapeDtypeStruct((planes, HALO, DEPTH), jnp.float32)
        for planes in (6 * PART + 2 * STEPS, 3 * MIDDLE, 3 * PLANES + 2 * STEPS)
    ]
    edge, middle, on_chip = pl.pallas_call(
        pack_kernel,
        out_shape=tuple(rims),
        in_specs=[IN_SMEM] + [IN_HBM] * 3 + [ANYWHERE],
        out_specs=(ANYWHERE,) * 3,
        scratch_shapes=[pltpu.SemaphoreType.DMA((16,))],
        compiler_params=pltpu.CompilerParams(vmem_limit_bytes=PACK_BYTES),
        name="pack",
    )(*args)
    count = lax.axis_size("dev")
    chips = [(i, i + 1) for i in range(1, count - 1, 2)]
    chips += [(j, i) for i, j in chips]
    cores = [(i, i + 1) for i in range(0, count, 2)]
    cores += [(j, i) for i, j in cores]
    edge = lax.ppermute(edge, "dev", chips)
    on_chip = lax.ppermute(on_chip, "dev", cores)
    middle = lax.ppermute(middle, "dev", chips)

    field, trace_high, trace_low = run_window("inner", 5, 3, 32, WINDOW_BYTES, args, (on_chip,))
    trace_high, trace_low = run_window("corner", 3, 2, 20, WINDOW_BYTES, args, (edge,), (trace_high, trace_low))

    subs = lax.axis_size("sub")
    up = [(i, i + 1) for i in range(subs - 1)]
    down = [(i + 1, i) for i in range(subs - 1)]
    new_left = lax.ppermute(trace_high, "sub", up)
    new_right = lax.ppermute(trace_low, "sub", down)
    (field,) = run_window("outer", 3, 2, 32, WINDOW_BYTES, args, (edge, middle), (field,), (trace_low,))
    return (field, new_left[None], new_right[None])


def solution(mesh):
    in_specs = (
        P("sub", "dev", None),
        P("sub", "dev", None),
        P("sub", "dev", None),
        P("sub", None, "dev", None),
        P("sub", None, "dev", None),
        P("sub"),
    )
    out_specs = (P("sub", "dev", None), P("sub", None, "dev", None), P("sub", None, "dev", None))
    return jax.shard_map(
        on_device, mesh=mesh, in_specs=in_specs, out_specs=out_specs, check_vma=False
    )
```
